256 devices in a mesh: pool: 32 (over y, x, core), tp: 8 (over z).
Axes of the slice: x: 4, y: 4, z: 8, core: 2. Of those that a mesh axis runs over, the one named last changes fastest.
Arguments:
- attended: bfloat16 [24576, 8192], P('pool', 'tp'), may hold values from -6 to 6
- out_weight: bfloat16 [8192, 4096], P('tp'), may hold values from -0.0625 to 0.0625
- cache_down: bfloat16 [384, 64, 8192], P('pool', None, 'tp'), may hold values from -0.0625 to 0.0625
- cache_up: bfloat16 [384, 64, 4096], P('pool', None, 'tp'), may hold values from -0.75 to 0.75
- pool_down: bfloat16 [256, 64, 8192], P('pool', None, 'tp'), may hold values from -0.0625 to 0.0625
- pool_up: bfloat16 [256, 64, 4096], P('pool', None, 'tp'), may hold values from -0.75 to 0.75
- segment_rows: int32 [32, 40], P('pool'), may hold values from 1 to 48, 768 in all within a row
- missed_slots: int32 [32, 28], P('pool'), may hold values from 0 to 39, as said below
- missed_ids: int32 [32, 28], replicated, may hold values from 0 to 255, as said below
- storage: int32 [256], replicated, may hold values from 0 to 255, as said below
Outputs:
- mixed: bfloat16 [24576, 4096], P('pool', 'tp')
The draws below stay inside these ranges and needn't reach their ends.
Inputs may be any that keep to these rules, and one draw needn't show every extreme that they name: A permutation: adapter a is kept at position storage[a], by owner storage[a] // 8 along pool. `missed_ids`: distinct adapters in each group; no owner keeps more than 2 of one group's missed adapters, and in every group some owner keeps exactly 2. `missed_slots`: distinct slots in each group, increasing. `segment_rows`: each group's entries sum to 768, the largest is 48.
All inputs are finite; a program needn't handle non-finite values.
Results may differ from the reference program's by a relative error of at most 0.0039.
Values may be sent and summed in bfloat16 or wider, within the bound.
A program may use at most 128 MiB of HBM per device.

```python
import math
import jax
import jax.numpy as jnp
import numpy as np
from jax import lax

D = 8192
D_OUT = 4096
R = 64
ROWS = 768
USED = 40
MISS = 28
ADP_DEV = 8
HITS = 12
NADAPT = 256
SEG_MAX = 48
CAP = 2
TOTAL_ROWS = 24576
N_POOL = 32


def miss_plan(key):
    storage = jax.random.permutation(jax.random.fold_in(key, 101), NADAPT).astype(jnp.int32)
    inverse = jnp.argsort(storage).astype(jnp.int32)
    weight_matrices = jax.random.randint(jax.random.fold_in(key, 102), (N_POOL,), 0, 4)
    preferred_adapter = jax.random.randint(jax.random.fold_in(key, 103), (), 0, N_POOL)
    request_adapters = N_POOL * CAP
    request_adapter_ids = jnp.arange(request_adapters, dtype=jnp.int32)
    holder_lookup = request_adapter_ids // CAP
    copy_of = request_adapter_ids % CAP

    def one_group(group_key):
        baseline_rating = jax.random.randint(jax.random.fold_in(group_key, 1), (request_adapters,), 0, 2 ** 20)
        shifts = jax.random.randint(jax.random.fold_in(group_key, 2), (N_POOL,), 0, ADP_DEV)
        extra_credit = weight_matrices[holder_lookup] * 2 ** 19 + (holder_lookup == preferred_adapter).astype(jnp.int32) * 2 ** 22
        adapter_rating = (baseline_rating + extra_credit) * request_adapters + request_adapter_ids
        unused, chosen = lax.top_k(adapter_rating, MISS)
        shuffle = jax.random.permutation(jax.random.fold_in(group_key, 3), MISS)
        chosen = chosen[shuffle]
        owners = holder_lookup[chosen]
        spots = owners * ADP_DEV + (copy_of[chosen] + shifts[owners]) % ADP_DEV
        return inverse[spots]
    group_keys = jax.random.split(jax.random.fold_in(key, 104), N_POOL)
    missed = jax.vmap(one_group)(group_keys).astype(jnp.int32)
    return (storage, missed)


def draw_storage(key, part):
    shared = miss_plan(key)
    return shared[0]


def draw_missed_ids(key, part):
    shared = miss_plan(key)
    return shared[1]


def draw_missed_slots(key, part):
    key = jax.random.fold_in(key, 9)
    group_keys = jax.random.split(key, N_POOL)

    def one_group(group_key):
        chosen = jax.random.permutation(group_key, USED)[:MISS]
        return jnp.sort(chosen).astype(jnp.int32)
    return jax.vmap(one_group)(group_keys).astype(jnp.int32)


def block_scale(rng, extent, shards, least, high):
    loudness = 1.0
    for dim, blocks in shards:
        steps = jax.random.uniform(jax.random.fold_in(jax.random.fold_in(rng, 6), dim), (blocks,), jnp.float32, least / len(shards), high / len(shards))
        loudness = loudness * jnp.repeat(jnp.exp(steps), extent[dim] // blocks).reshape((-1,) + (1,) * (len(extent) - 1 - dim))
    return loudness


def length_profile(amount, total, limit, slope):
    portions = [(1 << 20) // math.isqrt(rank ** slope) + 1 for rank in range(2, amount + 1)]
    rest, holding = total - limit - (amount - 1), [1] * (amount - 1)
    while rest > 0:
        candidates = [i for i in range(amount - 1) if holding[i] < limit]
        pool, remaining = sum([portions[i] for i in candidates]), rest
        for i in candidates:
            addition = min(limit - holding[i], max(1, remaining * portions[i] // pool), rest)
            holding[i] = holding[i] + addition
            rest = rest - addition
    return np.array([limit] + holding)


def uneven(key, number_of, total, reach, lean):
    if number_of == 2:
        one = jax.random.randint(key, (), max(1, total - reach), min(reach, total - 1) + 1)
        return jnp.stack([one, total - one])
    sizes = jnp.asarray(length_profile(number_of, total, reach, lean), jnp.int32)
    couples = (number_of - 1) // 2
    giver, sink = sizes[1:1 + 2 * couples:2], sizes[2:2 + 2 * couples:2]
    room = jnp.minimum(giver - 1, reach - sink)
    passed = jax.random.randint(jax.random.fold_in(key, 1), (couples,), 0, 1 << 20) % (room + 1)
    sizes = sizes.at[1:1 + 2 * couples:2].set(giver - passed).at[2:2 + 2 * couples:2].set(sink + passed)
    return sizes[jax.random.permutation(jax.random.fold_in(key, 2), number_of)]


def gaussian(key, extent, width, limit, shards=(), kind=jnp.bfloat16):
    array = width * jax.random.normal(key, extent, jnp.float32)
    if shards:
        array = array * block_scale(key, extent, shards, -0.22, 0.18)
    return jnp.clip(array, -limit, limit).astype(kind)


def setup_inputs(seed: int = 0) -> dict:
    arg_keys = jax.random.split(jax.random.key(seed), 11)
    return {
        "attended": gaussian(arg_keys[0], (TOTAL_ROWS, D), 1.0, 6.0, ((0, 32), (1, 8))),
        "out_weight": gaussian(arg_keys[1], (D, D_OUT), D ** -0.5, 0.0625, ((0, 8),)),
        "cache_down": gaussian(arg_keys[2], (N_POOL * HITS, R, D), D ** -0.5, 0.0625, ((0, 32), (2, 8))),
        "cache_up": gaussian(arg_keys[3], (N_POOL * HITS, R, D_OUT), R ** -0.5, 0.75, ((0, 32), (2, 8))),
        "pool_down": gaussian(arg_keys[4], (NADAPT, R, D), D ** -0.5, 0.0625, ((0, 32), (2, 8))),
        "pool_up": gaussian(arg_keys[5], (NADAPT, R, D_OUT), R ** -0.5, 0.75, ((0, 32), (2, 8))),
        "segment_rows": jax.vmap(lambda own: uneven(own, USED, ROWS, SEG_MAX, 2))(jax.random.split(arg_keys[6], N_POOL)).reshape((N_POOL, USED)).astype(jnp.int32),
        "missed_slots": draw_missed_slots(jax.random.fold_in(arg_keys[10], 71), 0),
        "missed_ids": draw_missed_ids(jax.random.fold_in(arg_keys[10], 71), 0),
        "storage": draw_storage(jax.random.fold_in(arg_keys[10], 71), 0),
    }


def slot_layout(lengths):
    row_ends = jnp.cumsum(lengths).astype(jnp.int32)
    row_starts = row_ends - lengths
    positions = jnp.arange(ROWS, dtype=jnp.int32)
    row_slot = jnp.sum((positions[:, None] >= row_ends[None, :]).astype(jnp.int32), axis=1)
    within = positions - row_starts[row_slot]
    flat_index = (row_slot * SEG_MAX + within).astype(jnp.int32)
    tile_steps = jnp.arange(SEG_MAX, dtype=jnp.int32)
    source = jnp.minimum(row_starts[:, None] + tile_steps[None, :], ROWS - 1).astype(jnp.int32)
    filled = tile_steps[None, :] < lengths[:, None]
    return source, filled, flat_index


def slot_order(missed):
    slots = jnp.arange(USED, dtype=jnp.int32)
    matches = missed[None, :] == slots[:, None]
    is_missed = jnp.any(matches, axis=1)
    miss_index = jnp.sum(jnp.where(matches, jnp.arange(MISS, dtype=jnp.int32)[None, :], 0), axis=1)
    hit_rank = jnp.cumsum(1 - is_missed.astype(jnp.int32)) - 1
    position = jnp.where(is_missed, HITS + miss_index, hit_rank).astype(jnp.int32)
    return position


def reference(attended, out_weight, cache_down, cache_up, pool_down, pool_up, segment_rows, missed_slots, missed_ids, storage):
    def one_group(own_group):
        local_rows = lax.dynamic_slice_in_dim(attended, own_group * ROWS, ROWS, 0)
        source, filled, flat_index = slot_layout(segment_rows[own_group])
        position = slot_order(missed_slots[own_group])
        stored = storage[missed_ids[own_group]]
        hit_down = lax.dynamic_slice_in_dim(cache_down, own_group * HITS, HITS, 0)
        hit_up = lax.dynamic_slice_in_dim(cache_up, own_group * HITS, HITS, 0)
        down_fac = jnp.concatenate([hit_down, pool_down[stored]], axis=0)[position]
        up_fac = jnp.concatenate([hit_up, pool_up[stored]], axis=0)[position]
        base = jnp.dot(local_rows, out_weight, preferred_element_type=jnp.float32)
        row_tiles = local_rows[source] * filled[:, :, None].astype(jnp.bfloat16)
        shrunk_tiles = jnp.einsum("usd,urd->usr", row_tiles.astype(jnp.float32), down_fac.astype(jnp.float32))
        shrunk = shrunk_tiles.reshape(USED * SEG_MAX, R)[flat_index].astype(jnp.bfloat16)
        low_tiles = shrunk[source] * filled[:, :, None].astype(jnp.bfloat16)
        grown_tiles = jnp.einsum("usr,urc->usc", low_tiles.astype(jnp.float32), up_fac.astype(jnp.float32))
        grown = grown_tiles.reshape(USED * SEG_MAX, D_OUT)[flat_index]
        return (base + grown).astype(jnp.bfloat16)

    stacked = lax.map(one_group, jnp.arange(N_POOL, dtype=jnp.int32))
    return stacked.reshape(N_POOL * ROWS, D_OUT)
```

```python
import functools

import jax
import jax.numpy as jnp
from jax import lax
from jax.experimental import pallas as pl
from jax.experimental.pallas import tpu as pltpu
from jax.sharding import PartitionSpec as P

USED = 40
MISS = 28
HITS = 12
ROWS = 768
KD = 1024
CHUNK = 512
HALF = 256
NZ = 8
BF = jnp.bfloat16
F32 = jnp.float32
MESH = pl.DeviceIdType.MESH
NT = (((1,), (1,)), ((), ()))


def kernel(
    att_h, w_h, cd_h, cu_h, pd_h, pu_h, seg, mslots, mids, stor,
    out_ref,
    att, w, cd, cu, sd, su, dd, du, rd, ru, zr, zs, base, prow, part, ar, own_sh, sh, sexp,
    pos, slot_s,
    in_sem, loc_sem, p1_s, p1_r, g_s, g_r, d_s, d_r, z_s, z_r, a_s, a_r,
):
    p = lax.axis_index("pool")
    z = lax.axis_index("tp")
    y, x, c = p // 8, (p // 2) % 4, p % 2
    member = (x * 2 + c, y * 2 + c)
    ring = (y, x)

    def device(mode, q):
        return y * 8 + q if mode == 0 else (q // 2) * 8 + x * 2 + q % 2

    def ring_next(mode, step):
        if mode == 0:
            return ((y + step) % 4) * 8 + x * 2 + c
        return y * 8 + ((x + step) % 4) * 2 + c

    def remote(src, dst, ss, rs, pool, tp):
        return pltpu.make_async_remote_copy(
            src_ref=src, dst_ref=dst, send_sem=ss, recv_sem=rs,
            device_id=(pool, tp), device_id_type=MESH,
        )

    sends = []

    loads = {}
    loads["att"] = pltpu.make_async_copy(att_h, att, in_sem.at[8])
    loads["cd"] = pltpu.make_async_copy(cd_h, cd, in_sem.at[9])
    loads["cu"] = pltpu.make_async_copy(cu_h, cu, in_sem.at[10])
    for k in range(NZ):
        d = (z + k) % NZ
        loads[k] = pltpu.make_async_copy(
            w_h.at[:, pl.ds(pl.multiple_of(d * CHUNK, CHUNK), CHUNK)], w.at[k], in_sem.at[k]
        )
    for k in ("att", 4, 3, 5, 2, 6, 1, 7, 0, "cd", "cu"):
        loads[k].start()

    bar = pltpu.get_barrier_semaphore()
    for mode in range(2):
        for o in range(1, 8):
            pl.semaphore_signal(
                bar, inc=1, device_id=(device(mode, (member[mode] + o) % 8), z), device_id_type=MESH
            )
    for o in range(1, NZ):
        pl.semaphore_signal(bar, inc=1, device_id=(p, (z + o) % NZ), device_id_type=MESH)
    pl.semaphore_wait(bar, 21)

    def spread_src(kind, mode, q):
        if kind == 0:
            return pd_h.at[:, pl.ds(32 * mode, 32), pl.ds(pl.multiple_of(q * 128, 128), 128)]
        return pu_h.at[
            :,
            pl.ds(pl.multiple_of(32 * mode + 16 * (q // 4), 16), 16),
            pl.ds(pl.multiple_of((q % 4) * 128, 128), 128),
        ]

    stock = (sd, su)

    def spread_dst(kind, mode, q):
        return stock[kind].at[mode, pl.ds(ring[mode] * 64 + q * 8, 8)]

    own_spread = {}

    def spread_start(kind):
        for o in (1, 7, 2, 6, 3, 5, 4):
            for mode in range(2):
                q = member[mode]
                t = (q + o) % 8
                cp = remote(
                    spread_src(kind, mode, t), spread_dst(kind, mode, q),
                    p1_s.at[mode, kind, o - 1], p1_r.at[mode, kind, o - 1], device(mode, t), z,
                )
                cp.start()
                sends.append(cp)
        for mode in range(2):
            q = member[mode]
            cp = pltpu.make_async_copy(
                spread_src(kind, mode, q), spread_dst(kind, mode, q), loc_sem.at[mode, kind]
            )
            cp.start()
            own_spread[mode, kind] = cp

    def spread_wait(kind, mode):
        q = member[mode]
        own_spread[mode, kind].wait()
        for o in range(1, 8):
            f = (q + 8 - o) % 8
            remote(
                spread_dst(kind, mode, f), spread_dst(kind, mode, f),
                p1_s.at[mode, kind, o - 1], p1_r.at[mode, kind, o - 1], device(mode, f), z,
            ).wait_recv()

    def shard(kind, mode, r, first, count):
        return stock[kind].at[mode, pl.ds(((ring[mode] + r) % 4) * 64 + first, count)]

    def gather_copy(kind, mode, i, ref):
        step = 1 if i % 2 == 0 else 3
        return remote(
            ref, ref, g_s.at[mode, kind, i], g_r.at[mode, kind, i], ring_next(mode, step), z
        )

    def gather_start(kind, mode):
        for i in range(2):
            cp = gather_copy(kind, mode, i, shard(kind, mode, 0, 0, 64))
            cp.start()
            sends.append(cp)

    def gather_forward(kind, mode):
        for i in range(2):
            r = 3 if i == 0 else 1
            got = shard(kind, mode, r, 0, 64)
            gather_copy(kind, mode, i, got).wait_recv()
            cp = gather_copy(kind, mode, 2 + i, shard(kind, mode, r, 32 * i, 32))
            cp.start()
            sends.append(cp)

    def gather_wait(kind, mode):
        for i in range(2):
            gather_copy(kind, mode, 2 + i, shard(kind, mode, 2, 32 * i, 32)).wait_recv()

    staged = (dd, du)
    got = (rd, ru)
    own_deliver = {}

    def positions():
        for mode in range(2):
            for q in range(8):
                g = device(mode, q)

                def one(j, carry, mode=mode, q=q, g=g):
                    s = stor[mids[g, j]]
                    if mode == 1:
                        s = ((s // 16) % 4) * 64 + (s // 64) * 16 + s % 16
                    pos[mode * 8 + q, j] = s
                    return carry

                lax.fori_loop(0, MISS, one, 0, unroll=4)

    def select(kind, mode, t, o):
        def one(j, carry):
            at = pos[mode * 8 + t, j]
            staged[kind][mode, o, j] = stock[kind][mode, at]
            return carry

        lax.fori_loop(0, MISS, one, 0, unroll=4)

    def deliver(kind):
        for o in (1, 7, 2, 6, 3, 5, 4, 0):
            for mode in range(2):
                q = member[mode]
                t = (q + o) % 8
                select(kind, mode, t, o)
                if o:
                    cp = remote(
                        staged[kind].at[mode, o], got[kind].at[mode, q],
                        d_s.at[mode, kind, o - 1], d_r.at[mode, kind, o - 1], device(mode, t), z,
                    )
                    cp.start()
                    sends.append(cp)
                else:
                    cp = pltpu.make_async_copy(
                        staged[kind].at[mode, o], got[kind].at[mode, q], loc_sem.at[mode, 2 + kind]
                    )
                    cp.start()
                    own_deliver[mode, kind] = cp

    def deliver_wait(kind, mode):
        q = member[mode]
        own_deliver[mode, kind].wait()
        for o in range(1, 8):
            f = (q + 8 - o) % 8
            remote(
                staged[kind].at[mode, o], got[kind].at[mode, f],
                d_s.at[mode, kind, o - 1], d_r.at[mode, kind, o - 1], device(mode, f), z,
            ).wait_recv()

    def ring_copy(way, k):
        to = (z + 1) % NZ if way == 0 else (z + NZ - 1) % NZ
        return remote(zs.at[way, k], zr.at[way, k], z_s.at[way, k], z_r.at[way, k], p, to)

    def ring_step(k):
        for way in range(2):
            dist = 4 - (k + 1) // 2
            d = dist if way == 0 else NZ - dist
            half = (k + way) % 2
            if k >= 2:
                ring_copy(way, k - 2).wait_recv()

            def tile(i, carry, d=d, half=half, way=way):
                rows = pl.ds(pl.multiple_of(i * 256, 256), 256)
                v = jnp.dot(
                    att[rows, :], w[d, :, HALF * half:HALF * half + HALF],
                    preferred_element_type=F32,
                )
                if k >= 2:
                    v = v + zr[way, k - 2, rows, :].astype(F32)
                zs[way, k, rows, :] = v.astype(BF)
                return carry

            lax.fori_loop(0, 3, tile, 0)
            cp = ring_copy(way, k)
            cp.start()
            sends.append(cp)

    def own_chunk():
        loads[0].wait()

        def tile(i, carry):
            rows = pl.ds(pl.multiple_of(i * 256, 256), 256)
            for half in range(2):
                cols = slice(HALF * half, HALF * half + HALF)
                base[rows, cols] = jnp.dot(
                    att[rows, :], w[0, :, cols], preferred_element_type=F32
                )
            return carry

        lax.fori_loop(0, 3, tile, 0)

    def row_positions():
        def one(s, carry):
            start, missed, hit = carry
            is_miss = jnp.logical_and(missed < MISS, mslots[0, jnp.minimum(missed, MISS - 1)] == s)
            slot_s[0, s] = start
            slot_s[1, s] = jnp.where(is_miss, HITS + missed, hit)
            step = jnp.where(is_miss, 1, 0)
            return start + seg[0, s], missed + step, hit + 1 - step

        lax.fori_loop(0, USED, one, (jnp.int32(0), jnp.int32(0), jnp.int32(0)))

        def tile(i, carry):
            rows = i * 96 + lax.broadcasted_iota(jnp.int32, (96, 128), 0)

            def slot(s, v):
                return jnp.where(rows >= slot_s[0, s], slot_s[1, s], v)

            prow[pl.ds(pl.multiple_of(i * 96, 96), 96), :] = lax.fori_loop(
                0, USED, slot, jnp.zeros((96, 128), jnp.int32), unroll=8
            )
            return carry

        lax.fori_loop(0, 8, tile, 0)

    def shrink():
        lane = lax.broadcasted_iota(jnp.int32, (384, 128), 1)
        packed = []
        for t in range(2):
            rows = slice(384 * t, 384 * t + 384)
            pm = prow[rows, :] - lane // 32
            a = att[rows, :]
            sums = []
            for mode in range(2):
                hit = cd[:, 32 * mode:32 * mode + 32, :].reshape(HITS * 32, KD)
                xh = lax.dot_general(a, hit, NT, preferred_element_type=F32)
                acc = jnp.zeros((384, 128), F32)
                for b in range(3):
                    acc = acc + jnp.where(pm == 4 * b, xh[:, 128 * b:128 * b + 128], 0.0)
                miss = jnp.concatenate(
                    [rd[mode, q].reshape(MISS * 32, 128) for q in range(8)], axis=1
                )
                xm = lax.dot_general(a, miss, NT, preferred_element_type=F32)
                for b in range(7):
                    acc = acc + jnp.where(
                        pm == HITS + 4 * b, xm[:, 128 * b:128 * b + 128], 0.0
                    )
                acc = acc + pltpu.roll(acc, 64, 1)
                acc = acc + pltpu.roll(acc, 32, 1)
                sums.append(acc)
            packed.append(jnp.where((lane // 32) % 2 == 0, sums[0], sums[1]))
        part[...] = jnp.where(lane < 64, packed[0], packed[1])

    def scatter_copy(o):
        t = (z + o) % NZ
        return remote(
            part.at[pl.ds(pl.multiple_of(t * 48, 16), 48)], ar.at[o - 1],
            a_s.at[0, o - 1], a_r.at[0, o - 1], p, t,
        )

    def ranks_copy(o, src):
        t = (z + o) % NZ
        dst = sh.at[pl.ds(pl.multiple_of(src * 48, 16), 48)]
        return remote(own_sh, dst, a_s.at[1, o - 1], a_r.at[1, o - 1], p, t)

    def own_ranks_copy():
        return pltpu.make_async_copy(
            own_sh, sh.at[pl.ds(pl.multiple_of(z * 48, 16), 48)], in_sem.at[11]
        )

    def rank_sums():
        order = (4, 3, 5, 2, 6, 1, 7)
        for o in order:
            cp = scatter_copy(o)
            cp.start()
            sends.append(cp)
        mine = pl.ds(pl.multiple_of(z * 48, 16), 48)
        total = part[mine, :]
        for o in (1, 7, 2, 6, 3, 5, 4):
            scatter_copy(o).wait_recv()
        for o in range(7):
            total = total + ar[o]
        own_sh[...] = total.astype(BF)
        own_ranks_copy().start()
        for o in order:
            cp = ranks_copy(o, z)
            cp.start()
            sends.append(cp)

    def ranks_wait():
        own_ranks_copy().wait()
        for o in (1, 7, 2, 6, 3, 5, 4):
            ranks_copy(o, (z + NZ - o) % NZ).wait_recv()

    def expand():
        lane = lax.broadcasted_iota(jnp.int32, (384, 128), 1)
        row_e = lax.broadcasted_iota(jnp.int32, (128, 512), 0)
        col_e = lax.broadcasted_iota(jnp.int32, (128, 512), 1)
        s = sh[...]
        for t in range(2):
            rows = slice(384 * t, 384 * t + 384)
            pick = row_e == 64 * t + (col_e // 128) * 16 + col_e % 16
            spread = jnp.dot(s, jnp.where(pick, 1.0, 0.0).astype(BF), preferred_element_type=F32)
            pm = prow[rows, :] - lane // 16
            for b in range(5):
                m = pm == 8 * b
                for rb in range(4):
                    sexp[rows, 640 * rb + 128 * b:640 * rb + 128 * b + 128] = jnp.where(
                        m, spread[:, 128 * rb:128 * rb + 128], 0.0
                    ).astype(BF)

    def grow():
        for rb in range(4):
            mode, first = rb // 2, (rb % 2) * 4
            up = jnp.concatenate(
                [
                    cu[:, 16 * rb:16 * rb + 16, :].reshape(HITS * 16, CHUNK),
                    jnp.concatenate(
                        [ru[mode, first + cb].reshape(MISS * 16, 128) for cb in range(4)], axis=1
                    ),
                ],
                axis=0,
            )
            for t in range(2):
                rows = slice(384 * t, 384 * t + 384)
                base[rows, :] += jnp.dot(
                    sexp[rows, 640 * rb:640 * rb + 640], up, preferred_element_type=F32
                )

    def finish():
        for way in range(2):
            for k in (5, 6):
                ring_copy(way, k).wait_recv()
        for half in range(2):
            cols = slice(HALF * half, HALF * half + HALF)
            k0 = 6 if half == 0 else 5
            out_ref[:, cols] = (
                base[:, cols]
                + zr[0, k0].astype(F32)
                + zr[1, 11 - k0].astype(F32)
            ).astype(BF)

    spread_start(0)
    loads["att"].wait()
    loads[4].wait()
    ring_step(0)
    spread_start(1)
    loads[3].wait()
    loads[5].wait()
    ring_step(1)
    positions()
    row_positions()
    for mode in range(2):
        spread_wait(0, mode)
        gather_start(0, mode)
    ring_step(2)
    for mode in range(2):
        spread_wait(1, mode)
        gather_start(1, mode)
    loads[2].wait()
    loads[6].wait()
    ring_step(3)
    for mode in range(2):
        gather_forward(0, mode)
    ring_step(4)
    for mode in range(2):
        gather_forward(1, mode)
    loads[1].wait()
    loads[7].wait()
    for mode in range(2):
        gather_wait(0, mode)
    deliver(0)
    ring_step(5)
    for mode in range(2):
        gather_wait(1, mode)
    deliver(1)
    ring_step(6)
    own_chunk()
    loads["cd"].wait()
    loads["cu"].wait()
    for mode in range(2):
        deliver_wait(0, mode)
    shrink()
    rank_sums()
    ranks_wait()
    expand()
    for mode in range(2):
        deliver_wait(1, mode)
    grow()
    finish()
    for cp in sends:
        cp.wait_send()


def per_device(*args):
    hbm = pl.BlockSpec(memory_space=pl.ANY)
    smem = pl.BlockSpec(memory_space=pltpu.SMEM)
    dma = pltpu.SemaphoreType.DMA
    return pl.pallas_call(
        kernel,
        out_shape=jax.ShapeDtypeStruct((ROWS, CHUNK), BF),
        in_specs=[hbm] * 6 + [smem] * 4,
        out_specs=pl.BlockSpec(memory_space=pltpu.VMEM),
        scratch_shapes=[
            pltpu.VMEM((ROWS, KD), BF),
            pltpu.VMEM((NZ, KD, CHUNK), BF),
            pltpu.VMEM((HITS, 64, KD), BF),
            pltpu.VMEM((HITS, 64, CHUNK), BF),
            pltpu.VMEM((2, 256, 32, 128), BF),
            pltpu.VMEM((2, 256, 16, 128), BF),
            pltpu.VMEM((2, 8, MISS, 32, 128), BF),
            pltpu.VMEM((2, 8, MISS, 16, 128), BF),
            pltpu.VMEM((2, 8, MISS, 32, 128), BF),
            pltpu.VMEM((2, 8, MISS, 16, 128), BF),
            pltpu.VMEM((2, 7, ROWS, HALF), BF),
            pltpu.VMEM((2, 7, ROWS, HALF), BF),
            pltpu.VMEM((ROWS, CHUNK), F32),
            pltpu.VMEM((ROWS, 128), jnp.int32),
            pltpu.VMEM((384, 128), F32),
            pltpu.VMEM((7, 48, 128), F32),
            pltpu.VMEM((48, 128), BF),
            pltpu.VMEM((384, 128), BF),
            pltpu.VMEM((ROWS, 2560), BF),
            pltpu.SMEM((16, MISS), jnp.int32),
            pltpu.SMEM((2, USED), jnp.int32),
            dma((12,)),
            dma((2, 4)),
            dma((2, 2, 7)),
            dma((2, 2, 7)),
            dma((2, 2, 4)),
            dma((2, 2, 4)),
            dma((2, 2, 7)),
            dma((2, 2, 7)),
            dma((2, 7)),
            dma((2, 7)),
            dma((2, 7)),
            dma((2, 7)),
        ],
        compiler_params=pltpu.CompilerParams(
            collective_id=0, has_side_effects=True, vmem_limit_bytes=60 * 1024 * 1024
        ),
        cost_estimate=pl.CostEstimate(
            flops=12_500_000_000, bytes_accessed=14_000_000, transcendentals=0
        ),
        name="lora_projection",
    )(*args)


def solution(mesh):
    return jax.shard_map(
        per_device,
        mesh=mesh,
        in_specs=(
            P("pool", "tp"),
            P("tp", None),
            P("pool", None, "tp"),
            P("pool", None, "tp"),
            P("pool", None, "tp"),
            P("pool", None, "tp"),
            P("pool", None),
            P("pool", None),
            P(),
            P(),
        ),
        out_specs=P("pool", "tp"),
        check_vma=False,
    )
```

```python
import functools

import jax
import jax.numpy as jnp
from jax import lax
from jax.experimental import pallas as pl
from jax.experimental.pallas import tpu as pltpu
from jax.sharding import PartitionSpec as P

USED = 40
MISS = 28
HITS = 12
ROWS = 768
KD = 1024
CHUNK = 512
HALF = 256
NZ = 8
BF = jnp.bfloat16
F32 = jnp.float32
MESH = pl.DeviceIdType.MESH
NT = (((1,), (1,)), ((), ()))


def kernel(
    att_h, w_h, cd_h, cu_h, pd_h, pu_h, seg_h, mslots_h, mids_h, stor_h,
    out_ref,
    att, w, cd, cu, pd, pu, sd, su, dd, du, rd, ru, zr, zs, base, prow, hacc, part, ar, own_sh, sh, sexp,
    seg, mslots, mids, stor, pos, slot_s,
    in_sem, loc_sem, p1_s, p1_r, g_s, g_r, d_s, d_r, z_s, z_r, a_s, a_r,
):
    p = lax.axis_index("pool")
    z = lax.axis_index("tp")
    y, x, c = p // 8, (p // 2) % 4, p % 2
    member = (x * 2 + c, y * 2 + c)
    ring = (y, x)

    def device(mode, q):
        return y * 8 + q if mode == 0 else (q // 2) * 8 + x * 2 + q % 2

    def ring_next(mode, step):
        if mode == 0:
            return ((y + step) % 4) * 8 + x * 2 + c
        return y * 8 + ((x + step) % 4) * 2 + c

    def remote(src, dst, ss, rs, pool, tp):
        return pltpu.make_async_remote_copy(
            src_ref=src, dst_ref=dst, send_sem=ss, recv_sem=rs,
            device_id=(pool, tp), device_id_type=MESH,
        )

    def partner(mode, e, back=False):
        place = (member[mode] // 2 + (4 - e // 2 if back else e // 2)) % 4
        return place * 2 + (c + e) % 2

    near_last = (4, 5, 2, 6, 3, 7, 1)
    sends = []

    bar = pltpu.get_barrier_semaphore()
    for mode in range(2):
        for o in range(1, 8):
            pl.semaphore_signal(
                bar, inc=1, device_id=(device(mode, partner(mode, o)), z), device_id_type=MESH
            )
    for o in range(1, NZ):
        pl.semaphore_signal(bar, inc=1, device_id=(p, (z + o) % NZ), device_id_type=MESH)

    loads = {}
    loads["att"] = pltpu.make_async_copy(att_h, att, in_sem.at[8])
    loads["cd"] = pltpu.make_async_copy(cd_h, cd, in_sem.at[9])
    loads["cu"] = pltpu.make_async_copy(cu_h, cu, in_sem.at[10])
    loads["pd"] = pltpu.make_async_copy(pd_h, pd, in_sem.at[12])
    loads["pu"] = pltpu.make_async_copy(pu_h, pu, in_sem.at[13])
    for k, (src, dst) in enumerate(
        ((seg_h, seg), (mslots_h, mslots), (mids_h, mids), (stor_h, stor))
    ):
        loads["int", k] = pltpu.make_async_copy(src, dst, in_sem.at[17 + k])
    for k in range(NZ):
        d = (z + k) % NZ
        loads[k] = pltpu.make_async_copy(
            w_h.at[:, pl.ds(pl.multiple_of(d * CHUNK, CHUNK), CHUNK)], w.at[k], in_sem.at[k]
        )
    for k in ("pd", "pu", "att", 4, 3, 5):
        loads[k].start()
    for k in range(4):
        loads["int", k].start()
    for k in (2, 6, 1, 7, 0, "cd", "cu"):
        loads[k].start()
    pl.semaphore_wait(bar, 21)

    def spread_src(kind, mode, q):
        if kind == 0:
            return pd.at[:, pl.ds(32 * mode, 32), pl.ds(pl.multiple_of(q * 128, 128), 128)]
        return pu.at[
            :,
            pl.ds(pl.multiple_of(32 * mode + 16 * (q // 4), 16), 16),
            pl.ds(pl.multiple_of((q % 4) * 128, 128), 128),
        ]

    stock = (sd, su)

    def spread_dst(kind, mode, q):
        return stock[kind].at[mode, pl.ds(ring[mode] * 64 + q * 8, 8)]

    own_spread = {}

    def spread_start(kind):
        for o in near_last:
            for mode in range(2):
                q = member[mode]
                t = partner(mode, o)
                cp = remote(
                    spread_src(kind, mode, t), spread_dst(kind, mode, q),
                    p1_s.at[mode, kind, o - 1], p1_r.at[mode, kind, o - 1], device(mode, t), z,
                )
                cp.start()
                sends.append(cp)
        for mode in range(2):
            q = member[mode]
            cp = pltpu.make_async_copy(
                spread_src(kind, mode, q), spread_dst(kind, mode, q), loc_sem.at[mode, kind]
            )
            cp.start()
            own_spread[mode, kind] = cp

    def spread_wait(kind, mode):
        q = member[mode]
        own_spread[mode, kind].wait()
        for o in range(1, 8):
            f = partner(mode, o, True)
            remote(
                spread_dst(kind, mode, f), spread_dst(kind, mode, f),
                p1_s.at[mode, kind, o - 1], p1_r.at[mode, kind, o - 1], device(mode, f), z,
            ).wait_recv()

    def shard(kind, mode, r, first, count):
        return stock[kind].at[mode, pl.ds(((ring[mode] + r) % 4) * 64 + first, count)]

    def gather_copy(kind, mode, i, ref):
        step = 1 if i % 2 == 0 else 3
        return remote(
            ref, ref, g_s.at[mode, kind, i], g_r.at[mode, kind, i], ring_next(mode, step), z
        )

    halves = ((0, 0), (0, 32), (0, 32), (0, 0), (3, 0), (1, 32))

    def gather_send(kind, mode, i):
        r, first = halves[i]
        cp = gather_copy(kind, mode, i, shard(kind, mode, r, first, 32))
        cp.start()
        sends.append(cp)

    def gather_recv(kind, mode, i):
        r, first = halves[i]
        r = (r + (3 if i % 2 == 0 else 1)) % 4
        gather_copy(kind, mode, i, shard(kind, mode, r, first, 32)).wait_recv()

    def gather_start(kind, mode):
        for i in range(4):
            gather_send(kind, mode, i)

    def gather_forward(kind, mode):
        for i in range(2):
            gather_recv(kind, mode, i)
            gather_send(kind, mode, 4 + i)

    def gather_wait(kind, mode):
        for i in range(2, 6):
            gather_recv(kind, mode, i)

    staged = (dd, du)
    got = (rd, ru)
    own_deliver = {}

    def positions():
        for mode in range(2):
            for q in range(8):
                g = device(mode, q)

                def one(j, carry, mode=mode, q=q, g=g):
                    s = stor[mids[g, j]]
                    if mode == 1:
                        s = ((s // 16) % 4) * 64 + (s // 64) * 16 + s % 16
                    pos[mode * 8 + q, j] = s
                    return carry

                lax.fori_loop(0, MISS, one, 0, unroll=14)

    def select(kind, mode, t, o):
        def one(j, carry):
            at = pos[mode * 8 + t, j]
            staged[kind][mode, o, j] = stock[kind][mode, at]
            return carry

        lax.fori_loop(0, MISS, one, 0, unroll=4)

    def deliver(kind, offsets):
        for o in offsets:
            for mode in range(2):
                q = member[mode]
                t = partner(mode, o)
                select(kind, mode, t, o)
                if o:
                    cp = remote(
                        staged[kind].at[mode, o], got[kind].at[mode, q],
                        d_s.at[mode, kind, o - 1], d_r.at[mode, kind, o - 1], device(mode, t), z,
                    )
                    cp.start()
                    sends.append(cp)
                else:
                    cp = pltpu.make_async_copy(
                        staged[kind].at[mode, o], got[kind].at[mode, q], loc_sem.at[mode, 2 + kind]
                    )
                    cp.start()
                    own_deliver[mode, kind] = cp

    def deliver_wait(kind, offsets):
        for o in offsets:
            for mode in range(2):
                if o == 0:
                    own_deliver[mode, kind].wait()
                    continue
                f = partner(mode, o, True)
                remote(
                    staged[kind].at[mode, o], got[kind].at[mode, f],
                    d_s.at[mode, kind, o - 1], d_r.at[mode, kind, o - 1], device(mode, f), z,
                ).wait_recv()

    def ring_copy(way, k, i):
        to = (z + 1) % NZ if way == 0 else (z + NZ - 1) % NZ
        rows = pl.ds(pl.multiple_of(i * 256, 256), 256)
        return remote(
            zs.at[way, k, rows], zr.at[way, k, rows], z_s.at[way, k, i], z_r.at[way, k, i], p, to
        )

    def ring_step(k, first=0, last=3):
        dist = 4 - (k + 1) // 2

        def tile(i, carry):
            rows = pl.ds(pl.multiple_of(i * 256, 256), 256)
            for way in range(2):
                d = dist if way == 0 else NZ - dist
                half = (k + way) % 2
                if k >= 2:
                    ring_copy(way, k - 2, i).wait_recv()
                v = jnp.dot(
                    att[rows, :], w[d, :, HALF * half:HALF * half + HALF],
                    preferred_element_type=F32,
                )
                if k >= 2:
                    v = v + zr[way, k - 2, rows, :].astype(F32)
                zs[way, k, rows, :] = v.astype(BF)
                ring_copy(way, k, i).start()
            return carry

        lax.fori_loop(first, last, tile, 0)

    def ring_drain():
        for k in range(7):
            for way in range(2):
                for i in range(3):
                    ring_copy(way, k, i).wait_send()

    def own_chunk():
        loads[0].wait()

        def tile(i, carry):
            rows = pl.ds(pl.multiple_of(i * 256, 256), 256)
            for half in range(2):
                cols = slice(HALF * half, HALF * half + HALF)
                base[rows, cols] = jnp.dot(
                    att[rows, :], w[0, :, cols], preferred_element_type=F32
                )
            return carry

        lax.fori_loop(0, 3, tile, 0)

    def row_positions():
        def one(s, carry):
            start, missed, hit = carry
            is_miss = jnp.logical_and(missed < MISS, mslots[0, jnp.minimum(missed, MISS - 1)] == s)
            slot_s[0, s] = start
            slot_s[1, s] = jnp.where(is_miss, HITS + missed, hit)
            step = jnp.where(is_miss, 1, 0)
            return start + seg[0, s], missed + step, hit + 1 - step

        lax.fori_loop(0, USED, one, (jnp.int32(0), jnp.int32(0), jnp.int32(0)))

        def tile(i, carry):
            rows = i * 96 + lax.broadcasted_iota(jnp.int32, (96, 128), 0)

            def slot(s, v):
                return jnp.where(rows >= slot_s[0, s], slot_s[1, s], v)

            prow[pl.ds(pl.multiple_of(i * 96, 96), 96), :] = lax.fori_loop(
                0, USED, slot, jnp.zeros((96, 128), jnp.int32), unroll=8
            )
            return carry

        lax.fori_loop(0, 8, tile, 0)

    def shrink_hits():
        lane = lax.broadcasted_iota(jnp.int32, (384, 128), 1)
        for t in range(2):
            rows = slice(384 * t, 384 * t + 384)
            pm = prow[rows, :] - lane // 32
            for mode in range(2):
                hit = cd[:, 32 * mode:32 * mode + 32, :].reshape(HITS * 32, KD)
                xh = lax.dot_general(att[rows, :], hit, NT, preferred_element_type=F32)
                acc = jnp.where(pm == 0, xh[:, 0:128], 0.0)
                for b in range(1, 3):
                    acc = acc + jnp.where(pm == 4 * b, xh[:, 128 * b:128 * b + 128], 0.0)
                hacc[mode, rows, :] = acc

    def shrink(i):
        lane = lax.broadcasted_iota(jnp.int32, (256, 128), 1)
        rows = slice(256 * i, 256 * i + 256)
        pm = prow[rows, :] - lane // 32
        sums = []
        for mode in range(2):
            acc = hacc[mode, rows, :]
            miss = jnp.concatenate(
                [rd[mode, q].reshape(MISS * 32, 128) for q in range(8)], axis=1
            )
            xm = lax.dot_general(att[rows, :], miss, NT, preferred_element_type=F32)
            for b in range(7):
                acc = acc + jnp.where(pm == HITS + 4 * b, xm[:, 128 * b:128 * b + 128], 0.0)
            acc = acc + pltpu.roll(acc, 64, 1)
            acc = acc + pltpu.roll(acc, 32, 1)
            sums.append(acc)
        full = jnp.where((lane // 32) % 2 == 0, sums[0], sums[1])
        part[i] = jnp.where(lane[0:128] < 64, full[0:128], full[128:256])
        for o in (4, 3, 5, 2, 6, 1, 7):
            cp = scatter_copy(i, o)
            cp.start()
            sends.append(cp)

    def scatter_copy(i, o):
        t = (z + o) % NZ
        return remote(
            part.at[i, pl.ds(pl.multiple_of(t * 16, 16), 16)], ar.at[i, o - 1],
            a_s.at[0, i, o - 1], a_r.at[0, i, o - 1], p, t,
        )

    def ranks_copy(i, o, src):
        t = (z + o) % NZ
        dst = sh.at[i, pl.ds(pl.multiple_of(src * 16, 16), 16)]
        return remote(own_sh.at[i], dst, a_s.at[1, i, o - 1], a_r.at[1, i, o - 1], p, t)

    def own_ranks_copy(i):
        return pltpu.make_async_copy(
            own_sh.at[i], sh.at[i, pl.ds(pl.multiple_of(z * 16, 16), 16)], in_sem.at[14 + i]
        )

    def rank_sums(i):
        total = part[i, pl.ds(pl.multiple_of(z * 16, 16), 16), :]
        for o in range(1, NZ):
            scatter_copy(i, o).wait_recv()
        for o in range(7):
            total = total + ar[i, o]
        own_sh[i] = total.astype(BF)
        own_ranks_copy(i).start()
        for o in (4, 3, 5, 2, 6, 1, 7):
            cp = ranks_copy(i, o, z)
            cp.start()
            sends.append(cp)

    def expand(i):
        own_ranks_copy(i).wait()
        for o in range(1, NZ):
            ranks_copy(i, o, (z + NZ - o) % NZ).wait_recv()
        lane = lax.broadcasted_iota(jnp.int32, (128, 128), 1)
        row_e = lax.broadcasted_iota(jnp.int32, (128, 512), 0)
        col_e = lax.broadcasted_iota(jnp.int32, (128, 512), 1)
        s = sh[i]
        for t in range(2):
            rows = slice(256 * i + 128 * t, 256 * i + 128 * t + 128)
            pick = row_e == 64 * t + (col_e // 128) * 16 + col_e % 16
            spread = jnp.dot(s, jnp.where(pick, 1.0, 0.0).astype(BF), preferred_element_type=F32)
            pm = prow[rows, :] - lane // 16
            for b in range(5):
                m = pm == 8 * b
                for rb in range(4):
                    sexp[rows, 640 * rb + 128 * b:640 * rb + 128 * b + 128] = jnp.where(
                        m, spread[:, 128 * rb:128 * rb + 128], 0.0
                    ).astype(BF)

    def grow(i):
        rows = slice(256 * i, 256 * i + 256)
        acc = base[rows, :]
        for rb in range(4):
            mode, first = rb // 2, (rb % 2) * 4
            up = jnp.concatenate(
                [
                    cu[:, 16 * rb:16 * rb + 16, :].reshape(HITS * 16, CHUNK),
                    jnp.concatenate(
                        [ru[mode, first + cb].reshape(MISS * 16, 128) for cb in range(4)], axis=1
                    ),
                ],
                axis=0,
            )
            acc = acc + jnp.dot(
                sexp[rows, 640 * rb:640 * rb + 640], up, preferred_element_type=F32
            )
        base[rows, :] = acc

    def finish(i):
        for way in range(2):
            for k in (5, 6):
                ring_copy(way, k, i).wait_recv()
        rows = slice(256 * i, 256 * i + 256)
        for half in range(2):
            cols = slice(HALF * half, HALF * half + HALF)
            k0 = 6 if half == 0 else 5
            out_ref[rows, cols] = (
                base[rows, cols]
                + zr[0, k0, rows, :].astype(F32)
                + zr[1, 11 - k0, rows, :].astype(F32)
            ).astype(BF)

    loads["pd"].wait()
    spread_start(0)
    loads["att"].wait()
    loads[4].wait()
    ring_step(0)
    loads["pu"].wait()
    spread_start(1)
    loads[3].wait()
    loads[5].wait()
    ring_step(1)
    for mode in range(2):
        spread_wait(0, mode)
        gather_start(0, mode)
    for k in range(4):
        loads["int", k].wait()
    positions()
    ring_step(2)
    for mode in range(2):
        gather_forward(0, mode)
    row_positions()
    for mode in range(2):
        spread_wait(1, mode)
    loads[2].wait()
    loads[6].wait()
    ring_step(3)
    for mode in range(2):
        gather_start(1, mode)
    for mode in range(2):
        gather_wait(0, mode)
    deliver(0, (4, 5, 2, 6, 3, 7, 1, 0))
    for mode in range(2):
        gather_forward(1, mode)
    ring_step(4)
    loads["cd"].wait()
    shrink_hits()
    own_chunk()
    loads[1].wait()
    loads[7].wait()
    ring_step(5)
    loads["cu"].wait()
    ring_step(6, 0, 2)
    for mode in range(2):
        gather_wait(1, mode)
    deliver_wait(0, (0, 1, 4, 5, 2))
    deliver(1, (4, 5, 2, 6, 3, 7, 1, 0))
    deliver_wait(0, (6, 3, 7))
    for i in range(3):
        shrink(i)
    for i in range(3):
        rank_sums(i)
    ring_step(6, 2, 3)
    expand(0)
    deliver_wait(1, range(8))
    grow(0)
    expand(1)
    grow(1)
    expand(2)
    grow(2)
    for i in range(3):
        finish(i)
    ring_drain()
    for cp in sends:
        cp.wait_send()


def per_device(*args):
    hbm = pl.BlockSpec(memory_space=pl.ANY)
    dma = pltpu.SemaphoreType.DMA
    return pl.pallas_call(
        kernel,
        out_shape=jax.ShapeDtypeStruct((ROWS, CHUNK), BF),
        in_specs=[hbm] * 10,
        out_specs=pl.BlockSpec(memory_space=pltpu.VMEM),
        scratch_shapes=[
            pltpu.VMEM((ROWS, KD), BF),
            pltpu.VMEM((NZ, KD, CHUNK), BF),
            pltpu.VMEM((HITS, 64, KD), BF),
            pltpu.VMEM((HITS, 64, CHUNK), BF),
            pltpu.VMEM((8, 64, KD), BF),
            pltpu.VMEM((8, 64, CHUNK), BF),
            pltpu.VMEM((2, 256, 32, 128), BF),
            pltpu.VMEM((2, 256, 16, 128), BF),
            pltpu.VMEM((2, 8, MISS, 32, 128), BF),
            pltpu.VMEM((2, 8, MISS, 16, 128), BF),
            pltpu.VMEM((2, 8, MISS, 32, 128), BF),
            pltpu.VMEM((2, 8, MISS, 16, 128), BF),
            pltpu.VMEM((2, 7, ROWS, HALF), BF),
            pltpu.VMEM((2, 7, ROWS, HALF), BF),
            pltpu.VMEM((ROWS, CHUNK), F32),
            pltpu.VMEM((ROWS, 128), jnp.int32),
            pltpu.VMEM((2, ROWS, 128), F32),
            pltpu.VMEM((3, 128, 128), F32),
            pltpu.VMEM((3, 7, 16, 128), F32),
            pltpu.VMEM((3, 16, 128), BF),
            pltpu.VMEM((3, 128, 128), BF),
            pltpu.VMEM((ROWS, 2560), BF),
            pltpu.SMEM((1, USED), jnp.int32),
            pltpu.SMEM((1, MISS), jnp.int32),
            pltpu.SMEM((32, MISS), jnp.int32),
            pltpu.SMEM((256,), jnp.int32),
            pltpu.SMEM((16, MISS), jnp.int32),
            pltpu.SMEM((2, USED), jnp.int32),
            dma((21,)),
            dma((2, 4)),
            dma((2, 2, 7)),
            dma((2, 2, 7)),
            dma((2, 2, 6)),
            dma((2, 2, 6)),
            dma((2, 2, 7)),
            dma((2, 2, 7)),
            dma((2, 7, 3)),
            dma((2, 7, 3)),
            dma((2, 3, 7)),
            dma((2, 3, 7)),
        ],
        compiler_params=pltpu.CompilerParams(
            collective_id=0, has_side_effects=True, vmem_limit_bytes=60 * 1024 * 1024
        ),
        cost_estimate=pl.CostEstimate(
            flops=12_500_000_000, bytes_accessed=14_000_000, transcendentals=0
        ),
        name="lora_projection",
    )(*args)


def solution(mesh):
    return jax.shard_map(
        per_device,
        mesh=mesh,
        in_specs=(
            P("pool", "tp"),
            P("tp", None),
            P("pool", None, "tp"),
            P("pool", None, "tp"),
            P("pool", None, "tp"),
            P("pool", None, "tp"),
            P("pool", None),
            P("pool", None),
            P(),
            P(),
        ),
        out_specs=P("pool", "tp"),
        check_vma=False,
    )
```

```python
import functools

import jax
import jax.numpy as jnp
from jax import lax
from jax.experimental import pallas as pl
from jax.experimental.pallas import tpu as pltpu
from jax.sharding import PartitionSpec as P

USED = 40
MISS = 28
HITS = 12
ROWS = 768
KD = 1024
CHUNK = 512
HALF = 256
NZ = 8
BF = jnp.bfloat16
F32 = jnp.float32
MESH = pl.DeviceIdType.MESH
NT = (((1,), (1,)), ((), ()))


def kernel(
    att_h, w_h, cd_h, cu_h, pd_h, pu_h, seg_h, mslots_h, mids_h, stor_h,
    out_ref,
    att, w, cd, cu, pd, pu, sd, su, dd, du, rd, ru, zr, zs, base, prow, hacc, part, ar, own_sh, sh, sexp,
    seg, mslots, mids, stor, pos, slot_s,
    out_v, in_sem, loc_sem, p1_s, p1_r, g_s, g_r, d_s, d_r, z_s, z_r, a_s, a_r,
):
    p = lax.axis_index("pool")
    z = lax.axis_index("tp")
    y, x, c = p // 8, (p // 2) % 4, p % 2
    member = (x * 2 + c, y * 2 + c)
    ring = (y, x)

    def device(mode, q):
        return y * 8 + q if mode == 0 else (q // 2) * 8 + x * 2 + q % 2

    def ring_next(mode, step):
        if mode == 0:
            return ((y + step) % 4) * 8 + x * 2 + c
        return y * 8 + ((x + step) % 4) * 2 + c

    def remote(src, dst, ss, rs, pool, tp):
        return pltpu.make_async_remote_copy(
            src_ref=src, dst_ref=dst, send_sem=ss, recv_sem=rs,
            device_id=(pool, tp), device_id_type=MESH,
        )

    def partner(mode, e, back=False):
        place = (member[mode] // 2 + (4 - e // 2 if back else e // 2)) % 4
        return place * 2 + (c + e) % 2

    near_last = (4, 5, 2, 6, 3, 7, 1)
    def await_recv(ref, sem):
        remote(ref, ref, z_s.at[0], sem, p, (z + 1) % NZ).wait_recv()

    def await_send(ref, sem):
        remote(ref, ref, sem, z_r.at[0], p, (z + 1) % NZ).wait_send()


    bar = pltpu.get_barrier_semaphore()
    for o in (4, 3, 5, 2, 6, 1, 7):
        pl.semaphore_signal(bar, inc=1, device_id=(p, (z + o) % NZ), device_id_type=MESH)
    for o in near_last:
        for mode in range(2):
            pl.semaphore_signal(
                bar, inc=1, device_id=(device(mode, partner(mode, o)), z), device_id_type=MESH
            )

    loads = {}
    for k, (src, dst) in enumerate(
        (
            (pd_h, pd), (pu_h, pu), (att_h, att), (cd_h, cd), (cu_h, cu),
            (seg_h, seg), (mslots_h, mslots), (mids_h, mids), (stor_h, stor),
        )
    ):
        loads[k] = pltpu.make_async_copy(src, dst, in_sem.at[k])

    def weight_copy(k):
        d = (z + k) % NZ
        return pltpu.make_async_copy(
            w_h.at[:, pl.ds(pl.multiple_of(d * CHUNK, CHUNK), CHUNK)],
            w.at[k], in_sem.at[9 if k == 4 else 10],
        )

    for k in range(3):
        loads[k].start()
    for k in (4, 3, 5, 2, 6, 1, 7, 0):
        weight_copy(k).start()
    for k in (5, 6, 7, 8, 3, 4):
        loads[k].start()
    pl.semaphore_wait(bar, 21)

    def spread_src(kind, mode, q):
        if kind == 0:
            return pd.at[:, pl.ds(32 * mode, 32), pl.ds(pl.multiple_of(q * 128, 128), 128)]
        return pu.at[
            :,
            pl.ds(pl.multiple_of(32 * mode + 16 * (q // 4), 16), 16),
            pl.ds(pl.multiple_of((q % 4) * 128, 128), 128),
        ]

    stock = (sd, su)

    def spread_dst(kind, mode, q):
        return stock[kind].at[mode, pl.ds(ring[mode] * 64 + q * 8, 8)]

    def spread_start(kind):
        for o in near_last:
            for mode in range(2):
                q = member[mode]
                t = partner(mode, o)
                remote(
                    spread_src(kind, mode, t), spread_dst(kind, mode, q),
                    p1_s.at[kind], p1_r.at[kind], device(mode, t), z,
                ).start()
        for mode in range(2):
            q = member[mode]
            pltpu.make_async_copy(
                spread_src(kind, mode, q), spread_dst(kind, mode, q), loc_sem.at[0, kind]
            ).start()

    def spread_wait(kind):
        both = stock[kind].at[0, pl.ds(0, 16)]
        pltpu.make_async_copy(both, both, loc_sem.at[0, kind]).wait()
        await_recv(stock[kind].at[0, pl.ds(0, 112)], p1_r.at[kind])

    def shard(kind, mode, r, first, count):
        return stock[kind].at[mode, pl.ds(((ring[mode] + r) % 4) * 64 + first, count)]

    def gather_copy(kind, mode, i, ref):
        step = 1 if i % 2 == 0 else 3
        return remote(
            ref, ref, g_s.at[kind], g_r.at[kind, 0 if i < 2 else 1], ring_next(mode, step), z
        )

    halves = ((0, 0), (0, 32), (0, 32), (0, 0), (3, 0), (1, 32))

    def gather_send(kind, i):
        r, first = halves[i]
        for mode in range(2):
            gather_copy(kind, mode, i, shard(kind, mode, r, first, 32)).start()

    def gather_start(kind):
        for i in range(4):
            gather_send(kind, i)

    def gather_forward(kind):
        await_recv(stock[kind].at[0, pl.ds(0, 128)], g_r.at[kind, 0])
        for i in range(4, 6):
            gather_send(kind, i)

    def gather_wait(kind):
        await_recv(stock[kind].at[0], g_r.at[kind, 1])

    staged = (dd, du)
    got = (rd, ru)

    def positions():
        for mode in range(2):
            for q in range(8):
                g = device(mode, q)

                def one(j, carry, mode=mode, q=q, g=g):
                    s = stor[mids[g, j]]
                    if mode == 1:
                        s = ((s // 16) % 4) * 64 + (s // 64) * 16 + s % 16
                    pos[mode * 8 + q, j] = s
                    return carry

                lax.fori_loop(0, MISS, one, 0, unroll=14)

    def select(kind, mode, t, o):
        def one(j, carry):
            at = pos[mode * 8 + t, j]
            staged[kind][mode, o, j] = stock[kind][mode, at]
            return carry

        lax.fori_loop(0, MISS, one, 0, unroll=14)

    def deliver(kind):
        for o in near_last + (0,):
            for mode in range(2):
                q = member[mode]
                t = partner(mode, o)
                select(kind, mode, t, o)
                src, dst = staged[kind].at[mode, o], got[kind].at[mode, q]
                if o:
                    remote(src, dst, d_s.at[kind], d_r.at[kind], device(mode, t), z).start()
                else:
                    pltpu.make_async_copy(src, dst, loc_sem.at[1, kind]).start()

    def deliver_wait(kind):
        both = staged[kind].at[0, pl.ds(0, 2)]
        pltpu.make_async_copy(both, both, loc_sem.at[1, kind]).wait()
        await_recv(staged[kind].at[:, pl.ds(1, 7)], d_r.at[kind])

    def ring_copy(way, k, i):
        to = (z + 1) % NZ if way == 0 else (z + NZ - 1) % NZ
        rows = pl.ds(pl.multiple_of(i * 256, 256), 256)
        return remote(
            zs.at[way, k, rows], zr.at[way, k, rows], z_s.at[0], z_r.at[k], p, to
        )

    def ring_step(k, first=0, last=3):
        dist = 4 - (k + 1) // 2
        if k >= 2 and first == 0:
            await_recv(zr.at[:, k - 2], z_r.at[k - 2])

        def tile(i, carry):
            rows = pl.ds(pl.multiple_of(i * 256, 256), 256)
            for way in range(2):
                d = dist if way == 0 else NZ - dist
                half = (k + way) % 2
                v = jnp.dot(
                    att[rows, :], w[d, :, HALF * half:HALF * half + HALF],
                    preferred_element_type=F32,
                )
                if k >= 2:
                    v = v + zr[way, k - 2, rows, :].astype(F32)
                zs[way, k, rows, :] = v.astype(BF)
                ring_copy(way, k, i).start()
            return carry

        lax.fori_loop(first, last, tile, 0)

    def own_chunk():

        def tile(i, carry):
            rows = pl.ds(pl.multiple_of(i * 256, 256), 256)
            for half in range(2):
                cols = slice(HALF * half, HALF * half + HALF)
                base[rows, cols] = jnp.dot(
                    att[rows, :], w[0, :, cols], preferred_element_type=F32
                )
            return carry

        lax.fori_loop(0, 3, tile, 0)

    def row_positions():
        def one(s, carry):
            start, missed, hit = carry
            is_miss = jnp.logical_and(missed < MISS, mslots[0, jnp.minimum(missed, MISS - 1)] == s)
            slot_s[0, s] = start
            slot_s[1, s] = jnp.where(is_miss, HITS + missed, hit)
            step = jnp.where(is_miss, 1, 0)
            return start + seg[0, s], missed + step, hit + 1 - step

        lax.fori_loop(0, USED, one, (jnp.int32(0), jnp.int32(0), jnp.int32(0)))

        def tile(i, carry):
            rows = i * 96 + lax.broadcasted_iota(jnp.int32, (96, 128), 0)

            def slot(s, v):
                return jnp.where(rows >= slot_s[0, s], slot_s[1, s], v)

            prow[pl.ds(pl.multiple_of(i * 96, 96), 96), :] = lax.fori_loop(
                0, USED, slot, jnp.zeros((96, 128), jnp.int32), unroll=8
            )
            return carry

        lax.fori_loop(0, 8, tile, 0)

    def shrink_hits():
        lane = lax.broadcasted_iota(jnp.int32, (384, 128), 1)
        for t in range(2):
            rows = slice(384 * t, 384 * t + 384)
            pm = prow[rows, :] - lane // 32
            for mode in range(2):
                hit = cd[:, 32 * mode:32 * mode + 32, :].reshape(HITS * 32, KD)
                xh = lax.dot_general(att[rows, :], hit, NT, preferred_element_type=F32)
                acc = jnp.where(pm == 0, xh[:, 0:128], 0.0)
                for b in range(1, 3):
                    acc = acc + jnp.where(pm == 4 * b, xh[:, 128 * b:128 * b + 128], 0.0)
                hacc[mode, rows, :] = acc

    def shrink(i):
        lane = lax.broadcasted_iota(jnp.int32, (256, 128), 1)
        rows = slice(256 * i, 256 * i + 256)
        pm = prow[rows, :] - lane // 32
        sums = []
        for mode in range(2):
            acc = hacc[mode, rows, :]
            miss = jnp.concatenate(
                [rd[mode, q].reshape(MISS * 32, 128) for q in range(8)], axis=1
            )
            xm = lax.dot_general(att[rows, :], miss, NT, preferred_element_type=F32)
            for b in range(7):
                acc = acc + jnp.where(pm == HITS + 4 * b, xm[:, 128 * b:128 * b + 128], 0.0)
            acc = acc + pltpu.roll(acc, 64, 1)
            acc = acc + pltpu.roll(acc, 32, 1)
            sums.append(acc)
        full = jnp.where((lane // 32) % 2 == 0, sums[0], sums[1])
        part[i] = jnp.where(lane[0:128] < 64, full[0:128], full[128:256])
        for o in (4, 3, 5, 2, 6, 1, 7):
            scatter_copy(i, o).start()

    def scatter_copy(i, o):
        t = (z + o) % NZ
        return remote(
            part.at[i, pl.ds(pl.multiple_of(t * 16, 16), 16)], ar.at[i, o - 1],
            a_s.at[0], a_r.at[0, i], p, t,
        )

    def ranks_copy(i, o, src):
        t = (z + o) % NZ
        dst = sh.at[i, pl.ds(pl.multiple_of(src * 16, 16), 16)]
        return remote(own_sh.at[i], dst, a_s.at[1], a_r.at[1, i], p, t)

    def own_ranks_copy(i):
        return pltpu.make_async_copy(
            own_sh.at[i], sh.at[i, pl.ds(pl.multiple_of(z * 16, 16), 16)], in_sem.at[11 + i]
        )

    def rank_sums(i):
        total = part[i, pl.ds(pl.multiple_of(z * 16, 16), 16), :]
        await_recv(ar.at[i], a_r.at[0, i])
        for o in range(7):
            total = total + ar[i, o]
        own_sh[i] = total.astype(BF)
        own_ranks_copy(i).start()
        for o in (4, 3, 5, 2, 6, 1, 7):
            ranks_copy(i, o, z).start()

    def expand(i):
        own_ranks_copy(i).wait()
        await_recv(su.at[0, pl.ds(0, 7)], a_r.at[1, i])
        lane = lax.broadcasted_iota(jnp.int32, (128, 128), 1)
        row_e = lax.broadcasted_iota(jnp.int32, (128, 512), 0)
        col_e = lax.broadcasted_iota(jnp.int32, (128, 512), 1)
        s = sh[i]
        for t in range(2):
            rows = slice(256 * i + 128 * t, 256 * i + 128 * t + 128)
            pick = row_e == 64 * t + (col_e // 128) * 16 + col_e % 16
            spread = jnp.dot(s, jnp.where(pick, 1.0, 0.0).astype(BF), preferred_element_type=F32)
            pm = prow[rows, :] - lane // 16
            for b in range(5):
                m = pm == 8 * b
                for rb in range(4):
                    sexp[rows, 640 * rb + 128 * b:640 * rb + 128 * b + 128] = jnp.where(
                        m, spread[:, 128 * rb:128 * rb + 128], 0.0
                    ).astype(BF)

    def grow(i):
        rows = slice(256 * i, 256 * i + 256)
        acc = base[rows, :]
        for rb in range(4):
            mode, first = rb // 2, (rb % 2) * 4
            up = jnp.concatenate(
                [
                    cu[:, 16 * rb:16 * rb + 16, :].reshape(HITS * 16, CHUNK),
                    jnp.concatenate(
                        [ru[mode, first + cb].reshape(MISS * 16, 128) for cb in range(4)], axis=1
                    ),
                ],
                axis=0,
            )
            acc = acc + jnp.dot(
                sexp[rows, 640 * rb:640 * rb + 640], up, preferred_element_type=F32
            )
        base[rows, :] = acc

    def out_copy(i):
        rows = pl.ds(256 * i, 256)
        return pltpu.make_async_copy(out_v.at[rows], out_ref.at[rows], in_sem.at[14 + i])

    def finish(i):
        rows = slice(256 * i, 256 * i + 256)
        for half in range(2):
            cols = slice(HALF * half, HALF * half + HALF)
            k0 = 6 if half == 0 else 5
            out_v[rows, cols] = (
                base[rows, cols]
                + zr[0, k0, rows, :].astype(F32)
                + zr[1, 11 - k0, rows, :].astype(F32)
            ).astype(BF)
        out_copy(i).start()

    def drain():
        for kind in range(2):
            await_send(stock[kind].at[0, pl.ds(0, 112)], p1_s.at[kind])
            await_send(stock[kind].at[:, pl.ds(0, 192)], g_s.at[kind])
            await_send(staged[kind].at[:, pl.ds(1, 7)], d_s.at[kind])
        await_send(zs, z_s.at[0])
        await_send(ar, a_s.at[0])
        await_send(su.at[0, pl.ds(0, 21)], a_s.at[1])
        for i in range(3):
            out_copy(i).wait()

    loads[0].wait()
    spread_start(0)
    loads[2].wait()
    weight_copy(4).wait()
    ring_step(0)
    loads[1].wait()
    spread_start(1)
    pltpu.make_async_copy(w.at[pl.ds(0, 7)], w.at[pl.ds(0, 7)], in_sem.at[10]).wait()
    ring_step(1)
    spread_wait(0)
    gather_start(0)
    for k in range(5, 9):
        loads[k].wait()
    positions()
    ring_step(2)
    gather_forward(0)
    row_positions()
    spread_wait(1)
    ring_step(3)
    gather_start(1)
    loads[3].wait()
    loads[4].wait()
    shrink_hits()
    own_chunk()
    gather_wait(0)
    deliver(0)
    gather_forward(1)
    ring_step(4)
    ring_step(5)
    ring_step(6, 0, 2)
    deliver_wait(0)
    shrink(0)
    gather_wait(1)
    deliver(1)
    shrink(1)
    shrink(2)
    rank_sums(0)
    rank_sums(1)
    ring_step(6, 2, 3)
    rank_sums(2)
    expand(0)
    deliver_wait(1)
    grow(0)
    expand(1)
    grow(1)
    expand(2)
    grow(2)
    await_recv(zr.at[:, 5], z_r.at[5])
    await_recv(zr.at[:, 6], z_r.at[6])
    for i in range(3):
        finish(i)
    drain()


def per_device(*args):
    hbm = pl.BlockSpec(memory_space=pl.ANY)
    dma = pltpu.SemaphoreType.DMA
    return pl.pallas_call(
        kernel,
        out_shape=jax.ShapeDtypeStruct((ROWS, CHUNK), BF),
        in_specs=[hbm] * 10,
        out_specs=hbm,
        scratch_shapes=[
            pltpu.VMEM((ROWS, KD), BF),
            pltpu.VMEM((NZ, KD, CHUNK), BF),
            pltpu.VMEM((HITS, 64, KD), BF),
            pltpu.VMEM((HITS, 64, CHUNK), BF),
            pltpu.VMEM((8, 64, KD), BF),
            pltpu.VMEM((8, 64, CHUNK), BF),
            pltpu.VMEM((2, 256, 32, 128), BF),
            pltpu.VMEM((2, 256, 16, 128), BF),
            pltpu.VMEM((2, 8, MISS, 32, 128), BF),
            pltpu.VMEM((2, 8, MISS, 16, 128), BF),
            pltpu.VMEM((2, 8, MISS, 32, 128), BF),
            pltpu.VMEM((2, 8, MISS, 16, 128), BF),
            pltpu.VMEM((2, 7, ROWS, HALF), BF),
            pltpu.VMEM((2, 7, ROWS, HALF), BF),
            pltpu.VMEM((ROWS, CHUNK), F32),
            pltpu.VMEM((ROWS, 128), jnp.int32),
            pltpu.VMEM((2, ROWS, 128), F32),
            pltpu.VMEM((3, 128, 128), F32),
            pltpu.VMEM((3, 7, 16, 128), F32),
            pltpu.VMEM((3, 16, 128), BF),
            pltpu.VMEM((3, 128, 128), BF),
            pltpu.VMEM((ROWS, 2560), BF),
            pltpu.SMEM((1, USED), jnp.int32),
            pltpu.SMEM((1, MISS), jnp.int32),
            pltpu.SMEM((32, MISS), jnp.int32),
            pltpu.SMEM((256,), jnp.int32),
            pltpu.SMEM((16, MISS), jnp.int32),
            pltpu.SMEM((2, USED), jnp.int32),
            pltpu.VMEM((ROWS, CHUNK), BF),
            dma((17,)),
            dma((2, 2)),
            dma((2,)),
            dma((2,)),
            dma((2,)),
            dma((2, 2)),
            dma((2,)),
            dma((2,)),
            dma((1,)),
            dma((7,)),
            dma((2,)),
            dma((2, 3)),
        ],
        compiler_params=pltpu.CompilerParams(
            collective_id=0, has_side_effects=True, vmem_limit_bytes=60 * 1024 * 1024
        ),
        cost_estimate=pl.CostEstimate(
            flops=12_500_000_000, bytes_accessed=14_000_000, transcendentals=0
        ),
        name="lora_projection",
    )(*args)


def solution(mesh):
    return jax.shard_map(
        per_device,
        mesh=mesh,
        in_specs=(
            P("pool", "tp"),
            P("tp", None),
            P("pool", None, "tp"),
            P("pool", None, "tp"),
            P("pool", None, "tp"),
            P("pool", None, "tp"),
            P("pool", None),
            P("pool", None),
            P(),
            P(),
        ),
        out_specs=P("pool", "tp"),
        check_vma=False,
    )
```

```python
import functools

import jax
import jax.numpy as jnp
from jax import lax
from jax.experimental import pallas as pl
from jax.experimental.pallas import tpu as pltpu
from jax.sharding import PartitionSpec as P

USED = 40
MISS = 28
HITS = 12
FIRST_MISS = 16
ROWS = 768
KD = 1024
CHUNK = 512
HALF = 256
NZ = 8
BF = jnp.bfloat16
F32 = jnp.float32
MESH = pl.DeviceIdType.MESH
NT = (((1,), (1,)), ((), ()))


def kernel(
    att_h, w_h, cd_h, cu_h, pd_h, pu_h, seg_h, mslots_h, mids_h, stor_h,
    out_ref,
    att, w, cd, cu, pd, pu, sd, su, dd, du, rd, ru, zr, zs, base, prow, hacc, part, ar, own_sh, sh, sexp_h, sexp_m, uh,
    seg, mslots, mids, stor, pos, slot_s,
    out_v, in_sem, loc_sem, p1_s, p1_r, g_s, g_r, d_s, d_r, z_s, z_r, a_s, a_r,
):
    p = lax.axis_index("pool")
    z = lax.axis_index("tp")
    y, x, c = p // 8, (p // 2) % 4, p % 2
    member = (x * 2 + c, y * 2 + c)
    ring = (y, x)

    def device(mode, q):
        return y * 8 + q if mode == 0 else (q // 2) * 8 + x * 2 + q % 2

    def ring_next(mode, step):
        if mode == 0:
            return ((y + step) % 4) * 8 + x * 2 + c
        return y * 8 + ((x + step) % 4) * 2 + c

    def remote(src, dst, ss, rs, pool, tp):
        return pltpu.make_async_remote_copy(
            src_ref=src, dst_ref=dst, send_sem=ss, recv_sem=rs,
            device_id=(pool, tp), device_id_type=MESH,
        )

    def partner(mode, e, back=False):
        place = (member[mode] // 2 + (4 - e // 2 if back else e // 2)) % 4
        return place * 2 + (c + e) % 2

    near_last = (4, 5, 2, 6, 3, 7, 1)
    def await_recv(ref, sem):
        remote(ref, ref, z_s.at[0], sem, p, (z + 1) % NZ).wait_recv()

    def await_send(ref, sem):
        remote(ref, ref, sem, z_r.at[0], p, (z + 1) % NZ).wait_send()


    bar = pltpu.get_barrier_semaphore()
    for o in (4, 3, 5, 2, 6, 1, 7):
        pl.semaphore_signal(bar, inc=1, device_id=(p, (z + o) % NZ), device_id_type=MESH)
    for o in near_last:
        for mode in range(2):
            pl.semaphore_signal(
                bar, inc=1, device_id=(device(mode, partner(mode, o)), z), device_id_type=MESH
            )

    loads = {}
    for k, (src, dst) in enumerate(
        (
            (pd_h, pd), (pu_h, pu), (att_h, att), (cd_h, cd), (cu_h, cu),
            (seg_h, seg), (mslots_h, mslots), (mids_h, mids), (stor_h, stor),
        )
    ):
        loads[k] = pltpu.make_async_copy(src, dst, in_sem.at[k])

    def weight_copy(k):
        d = (z + k) % NZ
        return pltpu.make_async_copy(
            w_h.at[:, pl.ds(pl.multiple_of(d * CHUNK, CHUNK), CHUNK)],
            w.at[k], in_sem.at[9 if k == 4 else 10],
        )

    for k in range(3):
        loads[k].start()
    for k in (4, 3, 5, 2, 6, 1, 7, 0):
        weight_copy(k).start()
    for k in (5, 6, 7, 8, 3, 4):
        loads[k].start()
    pl.semaphore_wait(bar, 21)

    def spread_src(kind, mode, q):
        if kind == 0:
            return pd.at[:, pl.ds(32 * mode, 32), pl.ds(pl.multiple_of(q * 128, 128), 128)]
        return pu.at[
            :,
            pl.ds(pl.multiple_of(32 * mode + 16 * (q // 4), 16), 16),
            pl.ds(pl.multiple_of((q % 4) * 128, 128), 128),
        ]

    stock = (sd, su)

    def spread_dst(kind, mode, q):
        return stock[kind].at[mode, pl.ds(ring[mode] * 64 + q * 8, 8)]

    def spread_start(kind):
        for o in near_last:
            for mode in range(2):
                q = member[mode]
                t = partner(mode, o)
                remote(
                    spread_src(kind, mode, t), spread_dst(kind, mode, q),
                    p1_s.at[kind], p1_r.at[kind], device(mode, t), z,
                ).start()
        for mode in range(2):
            q = member[mode]
            pltpu.make_async_copy(
                spread_src(kind, mode, q), spread_dst(kind, mode, q), loc_sem.at[0, kind]
            ).start()

    def spread_wait(kind):
        both = stock[kind].at[0, pl.ds(0, 16)]
        pltpu.make_async_copy(both, both, loc_sem.at[0, kind]).wait()
        await_recv(stock[kind].at[0, pl.ds(0, 112)], p1_r.at[kind])

    def shard(kind, mode, r, first, count):
        return stock[kind].at[mode, pl.ds(((ring[mode] + r) % 4) * 64 + first, count)]

    def gather_copy(kind, mode, i, ref):
        step = 1 if i % 2 == 0 else 3
        return remote(
            ref, ref, g_s.at[kind], g_r.at[kind, 0 if i < 2 else 1], ring_next(mode, step), z
        )

    halves = ((0, 0), (0, 32), (0, 32), (0, 0), (3, 0), (1, 32))

    def gather_send(kind, i):
        r, first = halves[i]
        for mode in range(2):
            gather_copy(kind, mode, i, shard(kind, mode, r, first, 32)).start()

    def gather_start(kind):
        for i in range(4):
            gather_send(kind, i)

    def gather_forward(kind):
        await_recv(stock[kind].at[0, pl.ds(0, 128)], g_r.at[kind, 0])
        for i in range(4, 6):
            gather_send(kind, i)

    def gather_wait(kind):
        await_recv(stock[kind].at[0], g_r.at[kind, 1])

    staged = (dd, du)
    got = (rd, ru)

    def positions():
        for mode in range(2):
            for q in range(8):
                g = device(mode, q)

                def one(j, carry, mode=mode, q=q, g=g):
                    s = stor[mids[g, j]]
                    if mode == 1:
                        s = ((s // 16) % 4) * 64 + (s // 64) * 16 + s % 16
                    pos[mode * 8 + q, j] = s
                    return carry

                lax.fori_loop(0, MISS, one, 0, unroll=14)

    def select(kind, mode, t, o):
        def one(j, carry):
            at = pos[mode * 8 + t, j]
            staged[kind][mode, o, j] = stock[kind][mode, at]
            return carry

        lax.fori_loop(0, MISS, one, 0, unroll=14)

    def deliver(kind, offsets=(4, 5, 2, 6, 3, 7, 1, 0)):
        for o in offsets:
            for mode in range(2):
                q = member[mode]
                t = partner(mode, o)
                select(kind, mode, t, o)
                src, dst = staged[kind].at[mode, o], got[kind].at[mode, q]
                if o:
                    remote(src, dst, d_s.at[kind], d_r.at[kind], device(mode, t), z).start()
                else:
                    pltpu.make_async_copy(src, dst, loc_sem.at[1, kind]).start()

    def deliver_wait(kind):
        both = staged[kind].at[0, pl.ds(0, 2)]
        pltpu.make_async_copy(both, both, loc_sem.at[1, kind]).wait()
        await_recv(staged[kind].at[:, pl.ds(1, 7)], d_r.at[kind])

    def ring_copy(way, k, i):
        to = (z + 1) % NZ if way == 0 else (z + NZ - 1) % NZ
        rows = pl.ds(pl.multiple_of(i * 256, 256), 256)
        return remote(
            zs.at[way, k, rows], zr.at[way, k, rows], z_s.at[0], z_r.at[k], p, to
        )

    def ring_step(k, first=0, last=3):
        dist = 4 - (k + 1) // 2
        if k >= 2 and first == 0:
            await_recv(zr.at[:, k - 2], z_r.at[k - 2])

        def tile(i, carry):
            rows = pl.ds(pl.multiple_of(i * 256, 256), 256)
            for way in range(2):
                d = dist if way == 0 else NZ - dist
                half = (k + way) % 2
                v = jnp.dot(
                    att[rows, :], w[d, :, HALF * half:HALF * half + HALF],
                    preferred_element_type=F32,
                )
                if k >= 2:
                    v = v + zr[way, k - 2, rows, :].astype(F32)
                zs[way, k, rows, :] = v.astype(BF)
                ring_copy(way, k, i).start()
            return carry

        lax.fori_loop(first, last, tile, 0)

    def own_chunk():

        def tile(i, carry):
            rows = pl.ds(pl.multiple_of(i * 256, 256), 256)
            for half in range(2):
                cols = slice(HALF * half, HALF * half + HALF)
                base[rows, cols] = jnp.dot(
                    att[rows, :], w[0, :, cols], preferred_element_type=F32
                )
            return carry

        lax.fori_loop(0, 3, tile, 0)

    def row_positions():
        def one(s, carry):
            start, missed, hit = carry
            is_miss = jnp.logical_and(missed < MISS, mslots[0, jnp.minimum(missed, MISS - 1)] == s)
            slot_s[0, s] = start
            slot_s[1, s] = jnp.where(is_miss, FIRST_MISS + missed, hit)
            step = jnp.where(is_miss, 1, 0)
            return start + seg[0, s], missed + step, hit + 1 - step

        lax.fori_loop(0, USED, one, (jnp.int32(0), jnp.int32(0), jnp.int32(0)))

        def tile(i, carry):
            rows = i * 96 + lax.broadcasted_iota(jnp.int32, (96, 128), 0)

            def slot(s, v):
                return jnp.where(rows >= slot_s[0, s], slot_s[1, s], v)

            prow[pl.ds(pl.multiple_of(i * 96, 96), 96), :] = lax.fori_loop(
                0, USED, slot, jnp.zeros((96, 128), jnp.int32), unroll=8
            )
            return carry

        lax.fori_loop(0, 8, tile, 0)

    def shrink_hits():
        lane = lax.broadcasted_iota(jnp.int32, (384, 128), 1)
        for t in range(2):
            rows = slice(384 * t, 384 * t + 384)
            pm = prow[rows, :] - lane // 32
            for mode in range(2):
                hit = cd[:, 32 * mode:32 * mode + 32, :].reshape(HITS * 32, KD)
                xh = lax.dot_general(att[rows, :], hit, NT, preferred_element_type=F32)
                acc = jnp.where(pm == 0, xh[:, 0:128], 0.0)
                for b in range(1, 3):
                    acc = acc + jnp.where(pm == 4 * b, xh[:, 128 * b:128 * b + 128], 0.0)
                hacc[mode, rows, :] = acc

    def shrink(i):
        lane = lax.broadcasted_iota(jnp.int32, (256, 128), 1)
        rows = slice(256 * i, 256 * i + 256)
        pm = prow[rows, :] - lane // 32
        sums = []
        for mode in range(2):
            acc = hacc[mode, rows, :]
            miss = jnp.concatenate(
                [rd[mode, q].reshape(MISS * 32, 128) for q in range(8)], axis=1
            )
            xm = lax.dot_general(att[rows, :], miss, NT, preferred_element_type=F32)
            for b in range(7):
                acc = acc + jnp.where(pm == FIRST_MISS + 4 * b, xm[:, 128 * b:128 * b + 128], 0.0)
            acc = acc + pltpu.roll(acc, 64, 1)
            acc = acc + pltpu.roll(acc, 32, 1)
            sums.append(acc)
        full = jnp.where((lane // 32) % 2 == 0, sums[0], sums[1])
        part[i] = jnp.where(lane[0:128] < 64, full[0:128], full[128:256])
        for o in (4, 3, 5, 2, 6, 1, 7):
            scatter_copy(i, o).start()

    def scatter_copy(i, o):
        t = (z + o) % NZ
        return remote(
            part.at[i, pl.ds(pl.multiple_of(t * 16, 16), 16)], ar.at[i, o - 1],
            a_s.at[0], a_r.at[0, i], p, t,
        )

    def ranks_copy(i, o, src):
        t = (z + o) % NZ
        dst = sh.at[i, pl.ds(pl.multiple_of(src * 16, 16), 16)]
        return remote(own_sh.at[i], dst, a_s.at[1], a_r.at[1, i], p, t)

    def own_ranks_copy(i):
        return pltpu.make_async_copy(
            own_sh.at[i], sh.at[i, pl.ds(pl.multiple_of(z * 16, 16), 16)], in_sem.at[11 + i]
        )

    def rank_sums(i):
        total = part[i, pl.ds(pl.multiple_of(z * 16, 16), 16), :]
        await_recv(ar.at[i], a_r.at[0, i])
        for o in range(7):
            total = total + ar[i, o]
        own_sh[i] = total.astype(BF)
        own_ranks_copy(i).start()
        for o in (4, 3, 5, 2, 6, 1, 7):
            ranks_copy(i, o, z).start()

    def expand(i):
        own_ranks_copy(i).wait()
        await_recv(su.at[0, pl.ds(0, 7)], a_r.at[1, i])
        lane = lax.broadcasted_iota(jnp.int32, (128, 128), 1)
        row_e = lax.broadcasted_iota(jnp.int32, (128, 512), 0)
        col_e = lax.broadcasted_iota(jnp.int32, (128, 512), 1)
        s = sh[i]
        for t in range(2):
            rows = slice(256 * i + 128 * t, 256 * i + 128 * t + 128)
            pick = row_e == 64 * t + (col_e // 128) * 16 + col_e % 16
            spread = jnp.dot(s, jnp.where(pick, 1.0, 0.0).astype(BF), preferred_element_type=F32)
            pm = prow[rows, :] - lane // 16
            for b in range(6):
                m = pm == 8 * b
                for rb in range(4):
                    v = jnp.where(m, spread[:, 128 * rb:128 * rb + 128], 0.0).astype(BF)
                    if b < 2:
                        sexp_h[rows, 256 * rb + 128 * b:256 * rb + 128 * b + 128] = v
                    else:
                        at = 512 * rb + 128 * (b - 2)
                        sexp_m[rows, at:at + 128] = v

    def up_hits():
        for rb in range(4):
            uh[256 * rb:256 * rb + 192, :] = cu[:, 16 * rb:16 * rb + 16, :].reshape(192, CHUNK)
            uh[256 * rb + 192:256 * rb + 256, :] = jnp.zeros((64, CHUNK), BF)

    def grow_hits(i):
        rows = slice(256 * i, 256 * i + 256)
        base[rows, :] += jnp.dot(sexp_h[rows, :], uh[...], preferred_element_type=F32)

    def out_copy(i):
        rows = pl.ds(256 * i, 256)
        return pltpu.make_async_copy(out_v.at[rows], out_ref.at[rows], in_sem.at[14 + i])

    def grow(i):
        rows = slice(256 * i, 256 * i + 256)
        acc = jnp.concatenate(
            [
                base[rows, 0:HALF] + zr[0, 6, rows, :].astype(F32) + zr[1, 5, rows, :].astype(F32),
                base[rows, HALF:] + zr[0, 5, rows, :].astype(F32) + zr[1, 6, rows, :].astype(F32),
            ],
            axis=1,
        )
        for rb in range(4):
            mode, first = rb // 2, (rb % 2) * 4
            up = jnp.concatenate(
                [
                    jnp.concatenate(
                        [ru[mode, first + cb].reshape(MISS * 16, 128) for cb in range(4)], axis=1
                    ),
                    jnp.zeros((64, CHUNK), BF),
                ],
                axis=0,
            )
            acc = acc + jnp.dot(
                sexp_m[rows, 512 * rb:512 * rb + 512], up, preferred_element_type=F32
            )
        out_v[rows, :] = acc.astype(BF)
        out_copy(i).start()

    def drain():
        for kind in range(2):
            await_send(stock[kind].at[0, pl.ds(0, 112)], p1_s.at[kind])
            await_send(stock[kind].at[:, pl.ds(0, 192)], g_s.at[kind])
            await_send(staged[kind].at[:, pl.ds(1, 7)], d_s.at[kind])
        await_send(zs, z_s.at[0])
        await_send(ar, a_s.at[0])
        await_send(su.at[0, pl.ds(0, 21)], a_s.at[1])
        for i in range(3):
            out_copy(i).wait()

    loads[0].wait()
    spread_start(0)
    loads[2].wait()
    weight_copy(4).wait()
    ring_step(0)
    loads[1].wait()
    spread_start(1)
    pltpu.make_async_copy(w.at[pl.ds(0, 7)], w.at[pl.ds(0, 7)], in_sem.at[10]).wait()
    ring_step(1)
    spread_wait(0)
    gather_start(0)
    for k in range(5, 9):
        loads[k].wait()
    positions()
    ring_step(2)
    gather_forward(0)
    row_positions()
    spread_wait(1)
    ring_step(3)
    gather_start(1)
    loads[3].wait()
    loads[4].wait()
    shrink_hits()
    own_chunk()
    up_hits()
    gather_wait(0)
    deliver(0)
    gather_forward(1)
    ring_step(4)
    ring_step(5)
    ring_step(6, 0, 2)
    deliver_wait(0)
    shrink(0)
    shrink(1)
    gather_wait(1)
    deliver(1)
    shrink(2)
    rank_sums(0)
    rank_sums(1)
    ring_step(6, 2, 3)
    rank_sums(2)
    for i in range(3):
        expand(i)
        grow_hits(i)
    deliver_wait(1)
    await_recv(zr.at[:, 5], z_r.at[5])
    await_recv(zr.at[:, 6], z_r.at[6])
    for i in range(3):
        grow(i)
    drain()


def per_device(*args):
    hbm = pl.BlockSpec(memory_space=pl.ANY)
    dma = pltpu.SemaphoreType.DMA
    return pl.pallas_call(
        kernel,
        out_shape=jax.ShapeDtypeStruct((ROWS, CHUNK), BF),
        in_specs=[hbm] * 10,
        out_specs=hbm,
        scratch_shapes=[
            pltpu.VMEM((ROWS, KD), BF),
            pltpu.VMEM((NZ, KD, CHUNK), BF),
            pltpu.VMEM((HITS, 64, KD), BF),
            pltpu.VMEM((HITS, 64, CHUNK), BF),
            pltpu.VMEM((8, 64, KD), BF),
            pltpu.VMEM((8, 64, CHUNK), BF),
            pltpu.VMEM((2, 256, 32, 128), BF),
            pltpu.VMEM((2, 256, 16, 128), BF),
            pltpu.VMEM((2, 8, MISS, 32, 128), BF),
            pltpu.VMEM((2, 8, MISS, 16, 128), BF),
            pltpu.VMEM((2, 8, MISS, 32, 128), BF),
            pltpu.VMEM((2, 8, MISS, 16, 128), BF),
            pltpu.VMEM((2, 7, ROWS, HALF), BF),
            pltpu.VMEM((2, 7, ROWS, HALF), BF),
            pltpu.VMEM((ROWS, CHUNK), F32),
            pltpu.VMEM((ROWS, 128), jnp.int32),
            pltpu.VMEM((2, ROWS, 128), F32),
            pltpu.VMEM((3, 128, 128), F32),
            pltpu.VMEM((3, 7, 16, 128), F32),
            pltpu.VMEM((3, 16, 128), BF),
            pltpu.VMEM((3, 128, 128), BF),
            pltpu.VMEM((ROWS, 1024), BF),
            pltpu.VMEM((ROWS, 2048), BF),
            pltpu.VMEM((1024, CHUNK), BF),
            pltpu.SMEM((1, USED), jnp.int32),
            pltpu.SMEM((1, MISS), jnp.int32),
            pltpu.SMEM((32, MISS), jnp.int32),
            pltpu.SMEM((256,), jnp.int32),
            pltpu.SMEM((16, MISS), jnp.int32),
            pltpu.SMEM((2, USED), jnp.int32),
            pltpu.VMEM((ROWS, CHUNK), BF),
            dma((17,)),
            dma((2, 2)),
            dma((2,)),
            dma((2,)),
            dma((2,)),
            dma((2, 2)),
            dma((2,)),
            dma((2,)),
            dma((1,)),
            dma((7,)),
            dma((2,)),
            dma((2, 3)),
        ],
        compiler_params=pltpu.CompilerParams(
            collective_id=0, has_side_effects=True, vmem_limit_bytes=60 * 1024 * 1024
        ),
        cost_estimate=pl.CostEstimate(
            flops=12_500_000_000, bytes_accessed=14_000_000, transcendentals=0
        ),
        name="lora_projection",
    )(*args)


def solution(mesh):
    return jax.shard_map(
        per_device,
        mesh=mesh,
        in_specs=(
            P("pool", "tp"),
            P("tp", None),
            P("pool", None, "tp"),
            P("pool", None, "tp"),
            P("pool", None, "tp"),
            P("pool", None, "tp"),
            P("pool", None),
            P("pool", None),
            P(),
            P(),
        ),
        out_specs=P("pool", "tp"),
        check_vma=False,
    )
```

```python
import functools

import jax
import jax.numpy as jnp
from jax import lax
from jax.experimental import pallas as pl
from jax.experimental.pallas import tpu as pltpu
from jax.sharding import PartitionSpec as P

USED = 40
MISS = 28
HITS = 12
FIRST_MISS = 16
ROWS = 768
KD = 1024
CHUNK = 512
HALF = 256
NZ = 8
BF = jnp.bfloat16
F32 = jnp.float32
MESH = pl.DeviceIdType.MESH
NT = (((1,), (1,)), ((), ()))


def kernel(
    att_h, w_h, cd_h, cu_h, pd_h, pu_h, seg_h, mslots_h, mids_h, stor_h,
    out_ref,
    att, w, cd, cu, pd, pu, sd, su, dd, du, rd, ru, zr, zs, base, prow, hacc, part, ar, own_sh, sh, sexp_h, sexp_m, uh,
    seg, mslots, mids, stor, pos, slot_s,
    out_v, in_sem, loc_sem, p1_s, p1_r, g_s, g_r, d_s, d_r, z_s, z_r, a_s, a_r,
):
    p = lax.axis_index("pool")
    z = lax.axis_index("tp")
    y, x, c = p // 8, (p // 2) % 4, p % 2
    member = (x * 2 + c, y * 2 + c)
    ring = (y, x)

    def device(mode, q):
        return y * 8 + q if mode == 0 else (q // 2) * 8 + x * 2 + q % 2

    def ring_next(mode, step):
        if mode == 0:
            return ((y + step) % 4) * 8 + x * 2 + c
        return y * 8 + ((x + step) % 4) * 2 + c

    def remote(src, dst, ss, rs, pool, tp):
        return pltpu.make_async_remote_copy(
            src_ref=src, dst_ref=dst, send_sem=ss, recv_sem=rs,
            device_id=(pool, tp), device_id_type=MESH,
        )

    def partner(mode, e, back=False):
        place = (member[mode] // 2 + (4 - e // 2 if back else e // 2)) % 4
        return place * 2 + (c + e) % 2

    near_last = (4, 5, 2, 6, 3, 7, 1)
    def await_recv(ref, sem):
        remote(ref, ref, z_s.at[0], sem, p, (z + 1) % NZ).wait_recv()

    def await_send(ref, sem):
        remote(ref, ref, sem, z_r.at[0], p, (z + 1) % NZ).wait_send()


    bar = pltpu.get_barrier_semaphore()
    for o in (4, 3, 5, 2, 6, 1, 7):
        pl.semaphore_signal(bar, inc=1, device_id=(p, (z + o) % NZ), device_id_type=MESH)
    for o in near_last:
        for mode in range(2):
            pl.semaphore_signal(
                bar, inc=1, device_id=(device(mode, partner(mode, o)), z), device_id_type=MESH
            )

    loads = {}
    for k, (src, dst) in enumerate(
        (
            (pd_h, pd), (pu_h, pu), (att_h, att), (cd_h, cd), (cu_h, cu),
            (seg_h, seg), (mslots_h, mslots), (mids_h, mids), (stor_h, stor),
        )
    ):
        loads[k] = pltpu.make_async_copy(src, dst, in_sem.at[k])

    def weight_copy(k):
        d = (z + k) % NZ
        return pltpu.make_async_copy(
            w_h.at[:, pl.ds(pl.multiple_of(d * CHUNK, CHUNK), CHUNK)],
            w.at[k], in_sem.at[9 if k == 4 else 10],
        )

    for k in range(3):
        loads[k].start()
    for k in (4, 3, 5, 2, 6, 1, 7, 0):
        weight_copy(k).start()
    for k in (5, 6, 7, 8, 3, 4):
        loads[k].start()
    pl.semaphore_wait(bar, 21)

    def spread_src(kind, mode, q):
        if kind == 0:
            return pd.at[:, pl.ds(32 * mode, 32), pl.ds(pl.multiple_of(q * 128, 128), 128)]
        return pu.at[
            :,
            pl.ds(pl.multiple_of(32 * mode + 16 * (q // 4), 16), 16),
            pl.ds(pl.multiple_of((q % 4) * 128, 128), 128),
        ]

    stock = (sd, su)

    def spread_dst(kind, mode, q):
        return stock[kind].at[mode, pl.ds(ring[mode] * 64 + q * 8, 8)]

    def spread_start(kind):
        for o in near_last:
            for mode in range(2):
                q = member[mode]
                t = partner(mode, o)
                remote(
                    spread_src(kind, mode, t), spread_dst(kind, mode, q),
                    p1_s.at[kind], p1_r.at[kind], device(mode, t), z,
                ).start()
        for mode in range(2):
            q = member[mode]
            pltpu.make_async_copy(
                spread_src(kind, mode, q), spread_dst(kind, mode, q), loc_sem.at[0, kind]
            ).start()

    def spread_wait(kind):
        both = stock[kind].at[0, pl.ds(0, 16)]
        pltpu.make_async_copy(both, both, loc_sem.at[0, kind]).wait()
        await_recv(stock[kind].at[0, pl.ds(0, 112)], p1_r.at[kind])

    def shard(kind, mode, r, first, count):
        return stock[kind].at[mode, pl.ds(((ring[mode] + r) % 4) * 64 + first, count)]

    def gather_copy(kind, mode, i, ref):
        step = 1 if i % 2 == 0 else 3
        return remote(
            ref, ref, g_s.at[kind], g_r.at[kind, 0 if i < 2 else 1], ring_next(mode, step), z
        )

    halves = ((0, 0), (0, 32), (0, 32), (0, 0), (3, 0), (1, 32))

    def gather_send(kind, i):
        r, first = halves[i]
        for mode in range(2):
            gather_copy(kind, mode, i, shard(kind, mode, r, first, 32)).start()

    def gather_start(kind):
        for i in range(4):
            gather_send(kind, i)

    def gather_forward(kind):
        await_recv(stock[kind].at[0, pl.ds(0, 128)], g_r.at[kind, 0])
        for i in range(4, 6):
            gather_send(kind, i)

    def gather_wait(kind):
        await_recv(stock[kind].at[0], g_r.at[kind, 1])

    staged = (dd, du)
    got = (rd, ru)

    def positions():
        for mode in range(2):
            for q in range(8):
                g = device(mode, q)

                def one(j, carry, mode=mode, q=q, g=g):
                    s = stor[mids[g, j]]
                    if mode == 1:
                        s = ((s // 16) % 4) * 64 + (s // 64) * 16 + s % 16
                    pos[mode * 8 + q, j] = s
                    return carry

                lax.fori_loop(0, MISS, one, 0, unroll=14)

    def select(kind, mode, t, o):
        def one(j, carry):
            at = pos[mode * 8 + t, j]
            staged[kind][mode, o, j] = stock[kind][mode, at]
            return carry

        lax.fori_loop(0, MISS, one, 0, unroll=14)

    def deliver(kind, offsets=(4, 5, 2, 6, 3, 7, 1, 0)):
        for o in offsets:
            for mode in range(2):
                q = member[mode]
                t = partner(mode, o)
                select(kind, mode, t, o)
                src, dst = staged[kind].at[mode, o], got[kind].at[mode, q]
                if o:
                    remote(src, dst, d_s.at[kind], d_r.at[kind], device(mode, t), z).start()
                else:
                    pltpu.make_async_copy(src, dst, loc_sem.at[1, kind]).start()

    def deliver_wait(kind):
        both = staged[kind].at[0, pl.ds(0, 2)]
        pltpu.make_async_copy(both, both, loc_sem.at[1, kind]).wait()
        await_recv(staged[kind].at[:, pl.ds(1, 7)], d_r.at[kind])

    def ring_copy(way, k, i):
        to = (z + 1) % NZ if way == 0 else (z + NZ - 1) % NZ
        rows = pl.ds(pl.multiple_of(i * 256, 256), 256)
        return remote(
            zs.at[way, k, rows], zr.at[way, k, rows], z_s.at[0], z_r.at[k], p, to
        )

    def ring_step(k, first=0, last=3):
        dist = 4 - (k + 1) // 2
        if k >= 2 and first == 0:
            await_recv(zr.at[:, k - 2], z_r.at[k - 2])

        def tile(i, carry):
            rows = pl.ds(pl.multiple_of(i * 256, 256), 256)
            for way in range(2):
                d = dist if way == 0 else NZ - dist
                half = (k + way) % 2
                v = jnp.dot(
                    att[rows, :], w[d, :, HALF * half:HALF * half + HALF],
                    preferred_element_type=F32,
                )
                if k >= 2:
                    v = v + zr[way, k - 2, rows, :].astype(F32)
                zs[way, k, rows, :] = v.astype(BF)
                ring_copy(way, k, i).start()
            return carry

        lax.fori_loop(first, last, tile, 0)

    def own_chunk():

        def tile(i, carry):
            rows = pl.ds(pl.multiple_of(i * 256, 256), 256)
            for half in range(2):
                cols = slice(HALF * half, HALF * half + HALF)
                base[rows, cols] = jnp.dot(
                    att[rows, :], w[0, :, cols], preferred_element_type=F32
                )
            return carry

        lax.fori_loop(0, 3, tile, 0)

    def row_positions():
        def one(s, carry):
            start, missed, hit = carry
            is_miss = jnp.logical_and(missed < MISS, mslots[0, jnp.minimum(missed, MISS - 1)] == s)
            slot_s[0, s] = start
            slot_s[1, s] = jnp.where(is_miss, FIRST_MISS + missed, hit)
            step = jnp.where(is_miss, 1, 0)
            return start + seg[0, s], missed + step, hit + 1 - step

        lax.fori_loop(0, USED, one, (jnp.int32(0), jnp.int32(0), jnp.int32(0)))

        def tile(i, carry):
            rows = i * 96 + lax.broadcasted_iota(jnp.int32, (96, 128), 0)

            def slot(s, v):
                return jnp.where(rows >= slot_s[0, s], slot_s[1, s], v)

            prow[pl.ds(pl.multiple_of(i * 96, 96), 96), :] = lax.fori_loop(
                0, USED, slot, jnp.zeros((96, 128), jnp.int32), unroll=8
            )
            return carry

        lax.fori_loop(0, 8, tile, 0)

    def shrink_hits():
        lane = lax.broadcasted_iota(jnp.int32, (384, 128), 1)
        for t in range(2):
            rows = slice(384 * t, 384 * t + 384)
            pm = prow[rows, :] - lane // 32
            for mode in range(2):
                hit = cd[:, 32 * mode:32 * mode + 32, :].reshape(HITS * 32, KD)
                xh = lax.dot_general(att[rows, :], hit, NT, preferred_element_type=F32)
                acc = jnp.where(pm == 0, xh[:, 0:128], 0.0)
                for b in range(1, 3):
                    acc = acc + jnp.where(pm == 4 * b, xh[:, 128 * b:128 * b + 128], 0.0)
                hacc[mode, rows, :] = acc

    def shrink(i):
        lane = lax.broadcasted_iota(jnp.int32, (256, 128), 1)
        rows = slice(256 * i, 256 * i + 256)
        pm = prow[rows, :] - lane // 32
        sums = []
        for mode in range(2):
            acc = hacc[mode, rows, :]
            miss = jnp.concatenate(
                [rd[mode, q].reshape(MISS * 32, 128) for q in range(8)], axis=1
            )
            xm = lax.dot_general(att[rows, :], miss, NT, preferred_element_type=F32)
            for b in range(7):
                acc = acc + jnp.where(pm == FIRST_MISS + 4 * b, xm[:, 128 * b:128 * b + 128], 0.0)
            acc = acc + pltpu.roll(acc, 64, 1)
            acc = acc + pltpu.roll(acc, 32, 1)
            sums.append(acc)
        full = jnp.where((lane // 32) % 2 == 0, sums[0], sums[1])
        part[i] = jnp.where(lane[0:128] < 64, full[0:128], full[128:256])
        for o in (4, 3, 5, 2, 6, 1, 7):
            scatter_copy(i, o).start()

    def scatter_copy(i, o):
        t = (z + o) % NZ
        return remote(
            part.at[i, pl.ds(pl.multiple_of(t * 16, 16), 16)], ar.at[i, o - 1],
            a_s.at[0], a_r.at[0, i], p, t,
        )

    def ranks_copy(i, o, src):
        t = (z + o) % NZ
        dst = sh.at[i, pl.ds(pl.multiple_of(src * 16, 16), 16)]
        return remote(own_sh.at[i], dst, a_s.at[1], a_r.at[1, i], p, t)

    def own_ranks_copy(i):
        return pltpu.make_async_copy(
            own_sh.at[i], sh.at[i, pl.ds(pl.multiple_of(z * 16, 16), 16)], in_sem.at[11 + i]
        )

    def rank_sums(i):
        total = part[i, pl.ds(pl.multiple_of(z * 16, 16), 16), :]
        await_recv(ar.at[i], a_r.at[0, i])
        for o in range(7):
            total = total + ar[i, o]
        own_sh[i] = total.astype(BF)
        own_ranks_copy(i).start()
        for o in (4, 3, 5, 2, 6, 1, 7):
            ranks_copy(i, o, z).start()

    def expand(i):
        own_ranks_copy(i).wait()
        await_recv(su.at[0, pl.ds(0, 7)], a_r.at[1, i])
        lane = lax.broadcasted_iota(jnp.int32, (128, 128), 1)
        row_e = lax.broadcasted_iota(jnp.int32, (128, 512), 0)
        col_e = lax.broadcasted_iota(jnp.int32, (128, 512), 1)
        s = sh[i]
        for t in range(2):
            rows = slice(256 * i + 128 * t, 256 * i + 128 * t + 128)
            pick = row_e == 64 * t + (col_e // 128) * 16 + col_e % 16
            spread = jnp.dot(s, jnp.where(pick, 1.0, 0.0).astype(BF), preferred_element_type=F32)
            pm = prow[rows, :] - lane // 16
            for b in range(6):
                m = pm == 8 * b
                for rb in range(4):
                    v = jnp.where(m, spread[:, 128 * rb:128 * rb + 128], 0.0).astype(BF)
                    if b < 2:
                        sexp_h[rows, 256 * rb + 128 * b:256 * rb + 128 * b + 128] = v
                    else:
                        at = 512 * rb + 128 * (b - 2)
                        sexp_m[rows, at:at + 128] = v

    def up_hits():
        for rb in range(4):
            uh[256 * rb:256 * rb + 192, :] = cu[:, 16 * rb:16 * rb + 16, :].reshape(192, CHUNK)
            uh[256 * rb + 192:256 * rb + 256, :] = jnp.zeros((64, CHUNK), BF)

    def grow_hits(i):
        rows = slice(256 * i, 256 * i + 256)
        base[rows, :] += jnp.dot(sexp_h[rows, :], uh[...], preferred_element_type=F32)

    def out_copy(i):
        rows = pl.ds(256 * i, 256)
        return pltpu.make_async_copy(out_v.at[rows], out_ref.at[rows], in_sem.at[14 + i])

    def grow(i):
        rows = slice(256 * i, 256 * i + 256)
        acc = jnp.concatenate(
            [
                base[rows, 0:HALF] + zr[0, 6, rows, :].astype(F32) + zr[1, 5, rows, :].astype(F32),
                base[rows, HALF:] + zr[0, 5, rows, :].astype(F32) + zr[1, 6, rows, :].astype(F32),
            ],
            axis=1,
        )
        for rb in range(4):
            mode, first = rb // 2, (rb % 2) * 4
            up = jnp.concatenate(
                [
                    jnp.concatenate(
                        [ru[mode, first + cb].reshape(MISS * 16, 128) for cb in range(4)], axis=1
                    ),
                    jnp.zeros((64, CHUNK), BF),
                ],
                axis=0,
            )
            acc = acc + jnp.dot(
                sexp_m[rows, 512 * rb:512 * rb + 512], up, preferred_element_type=F32
            )
        out_v[rows, :] = acc.astype(BF)
        out_copy(i).start()

    def drain():
        for kind in range(2):
            await_send(stock[kind].at[0, pl.ds(0, 112)], p1_s.at[kind])
            await_send(stock[kind].at[:, pl.ds(0, 192)], g_s.at[kind])
            await_send(staged[kind].at[:, pl.ds(1, 7)], d_s.at[kind])
        await_send(zs, z_s.at[0])
        await_send(ar, a_s.at[0])
        await_send(su.at[0, pl.ds(0, 21)], a_s.at[1])
        for i in range(3):
            out_copy(i).wait()

    loads[0].wait()
    spread_start(0)
    loads[2].wait()
    weight_copy(4).wait()
    ring_step(0)
    loads[1].wait()
    spread_start(1)
    pltpu.make_async_copy(w.at[pl.ds(0, 7)], w.at[pl.ds(0, 7)], in_sem.at[10]).wait()
    ring_step(1)
    spread_wait(0)
    gather_start(0)
    for k in range(5, 9):
        loads[k].wait()
    positions()
    ring_step(2)
    gather_forward(0)
    row_positions()
    spread_wait(1)
    ring_step(3)
    gather_start(1)
    loads[3].wait()
    loads[4].wait()
    shrink_hits()
    own_chunk()
    up_hits()
    gather_wait(0)
    deliver(0)
    gather_forward(1)
    ring_step(4)
    ring_step(5)
    ring_step(6, 0, 2)
    deliver_wait(0)
    shrink(0)
    shrink(1)
    gather_wait(1)
    deliver(1)
    shrink(2)
    rank_sums(0)
    rank_sums(1)
    rank_sums(2)
    ring_step(6, 2, 3)
    for i in range(3):
        expand(i)
        grow_hits(i)
    deliver_wait(1)
    await_recv(zr.at[:, 5], z_r.at[5])
    await_recv(zr.at[:, 6], z_r.at[6])
    for i in range(3):
        grow(i)
    drain()


def per_device(*args):
    hbm = pl.BlockSpec(memory_space=pl.ANY)
    dma = pltpu.SemaphoreType.DMA
    return pl.pallas_call(
        kernel,
        out_shape=jax.ShapeDtypeStruct((ROWS, CHUNK), BF),
        in_specs=[hbm] * 10,
        out_specs=hbm,
        scratch_shapes=[
            pltpu.VMEM((ROWS, KD), BF),
            pltpu.VMEM((NZ, KD, CHUNK), BF),
            pltpu.VMEM((HITS, 64, KD), BF),
            pltpu.VMEM((HITS, 64, CHUNK), BF),
            pltpu.VMEM((8, 64, KD), BF),
            pltpu.VMEM((8, 64, CHUNK), BF),
            pltpu.VMEM((2, 256, 32, 128), BF),
            pltpu.VMEM((2, 256, 16, 128), BF),
            pltpu.VMEM((2, 8, MISS, 32, 128), BF),
            pltpu.VMEM((2, 8, MISS, 16, 128), BF),
            pltpu.VMEM((2, 8, MISS, 32, 128), BF),
            pltpu.VMEM((2, 8, MISS, 16, 128), BF),
            pltpu.VMEM((2, 7, ROWS, HALF), BF),
            pltpu.VMEM((2, 7, ROWS, HALF), BF),
            pltpu.VMEM((ROWS, CHUNK), F32),
            pltpu.VMEM((ROWS, 128), jnp.int32),
            pltpu.VMEM((2, ROWS, 128), F32),
            pltpu.VMEM((3, 128, 128), F32),
            pltpu.VMEM((3, 7, 16, 128), F32),
            pltpu.VMEM((3, 16, 128), BF),
            pltpu.VMEM((3, 128, 128), BF),
            pltpu.VMEM((ROWS, 1024), BF),
            pltpu.VMEM((ROWS, 2048), BF),
            pltpu.VMEM((1024, CHUNK), BF),
            pltpu.SMEM((1, USED), jnp.int32),
            pltpu.SMEM((1, MISS), jnp.int32),
            pltpu.SMEM((32, MISS), jnp.int32),
            pltpu.SMEM((256,), jnp.int32),
            pltpu.SMEM((16, MISS), jnp.int32),
            pltpu.SMEM((2, USED), jnp.int32),
            pltpu.VMEM((ROWS, CHUNK), BF),
            dma((17,)),
            dma((2, 2)),
            dma((2,)),
            dma((2,)),
            dma((2,)),
            dma((2, 2)),
            dma((2,)),
            dma((2,)),
            dma((1,)),
            dma((7,)),
            dma((2,)),
            dma((2, 3)),
        ],
        compiler_params=pltpu.CompilerParams(
            collective_id=0, has_side_effects=True, vmem_limit_bytes=60 * 1024 * 1024
        ),
        cost_estimate=pl.CostEstimate(
            flops=12_500_000_000, bytes_accessed=14_000_000, transcendentals=0
        ),
        name="lora_projection",
    )(*args)


def solution(mesh):
    return jax.shard_map(
        per_device,
        mesh=mesh,
        in_specs=(
            P("pool", "tp"),
            P("tp", None),
            P("pool", None, "tp"),
            P("pool", None, "tp"),
            P("pool", None, "tp"),
            P("pool", None, "tp"),
            P("pool", None),
            P("pool", None),
            P(),
            P(),
        ),
        out_specs=P("pool", "tp"),
        check_vma=False,
    )
```
